32 devices in a mesh: dp: 16 (over z, x, core), slab: 2 (over y).
Axes of the slice: x: 2, y: 2, z: 4, core: 2. Of those that a mesh axis runs over, the one named last changes fastest.
Arguments:
- point_feats: bfloat16 [16, 8, 64, 128], P('dp', 'slab'), may hold values from -6 to 6
- point_coords: bfloat16 [16, 8, 3, 128], P('dp', 'slab'), may hold values from 0 to 1
- slot_block: int32 [16, 2, 2, 4], P('dp', 'slab'), may hold values from 0 to 3
- slot_cell: int32 [16, 2, 2, 4], P('dp', 'slab'), may hold values from 0 to 8191, as said below
- slot_count: int32 [16, 2, 2], P('dp', 'slab'), may hold values from 1 to 4, as said below
- cotangent: float32 [16, 16, 16, 16, 128], P('dp', 'slab'), may hold values from -6 to 6
- offset_map: float32 [64, 3], replicated, may hold values from -12 to 12
- offset_bias: float32 [64], replicated, may hold values from -4 to 4
- kernel_mix: bfloat16 [64, 64, 64], replicated, may hold values from -0.75 to 0.75
- lift_weight: bfloat16 [64, 64], replicated, may hold values from -0.75 to 0.75
Outputs:
- spectral_grad: float32 [64, 16, 16, 16, 128], P('dp', 'slab')
The draws below stay inside these ranges and needn't reach their ends.
Inputs may be any that keep to these rules, and one draw needn't show every extreme that they name: `slot_cell`: cell row of a slot on its receiving slab index. `slot_count`: in every sample one receiving slab index, drawn from the seed, gets 4 live slots from every sending slab index.
All inputs are finite; a program needn't handle non-finite values.
Results may differ from the reference program's by a relative error of at most 0.0031.
Values may be sent and summed in bfloat16 or wider, within the bound.
No kernel may reach another device: no remote copies, remote signals or barrier semaphores. Data moves between devices by JAX's collectives and lax.ppermute only.
A program may use at most 128 MiB of HBM per device.

```python
import math
import jax
import jax.numpy as jnp
from jax import lax

C = 64
GX = 128
GY = 128
GZ = 128
KM = 16
BP = 128
KH = 64
CAP = 4
XL = 64
PB_DEV = 4
PBLOCKS = 8
SAMPLES = 16
N_SLAB = 2


def draw_slot_cell(key, part):
    pool_size = max(2, N_SLAB * CAP // 2)
    pool = jax.random.randint(jax.random.fold_in(key, 11), (SAMPLES, 1, N_SLAB, pool_size), 0, XL * GY)
    pool = pool.at[:, :, :, 0].set(XL * GY - 1)
    pool = pool.at[:, :, :, 1].set(0)
    picks = jax.random.randint(jax.random.fold_in(key, 12), (SAMPLES, N_SLAB, N_SLAB, CAP), 0, pool_size)
    picks = picks.at[:, 0, :, 0].set(0)
    picks = picks.at[:, 1, :, 0].set(1)
    pool_all = jnp.broadcast_to(pool, (SAMPLES, N_SLAB, N_SLAB, pool_size))
    return jnp.take_along_axis(pool_all, picks, axis=3).astype(jnp.int32)


def draw_slot_count(key, part):
    upper = max(2, CAP * 2 // 3 + 1)
    base_count = jax.random.randint(jax.random.fold_in(key, 21), (SAMPLES, N_SLAB, N_SLAB), 1, upper)
    hottest = jax.random.randint(jax.random.fold_in(key, 22), (SAMPLES, 1, 1), 0, N_SLAB)
    receivers = jnp.arange(N_SLAB)[None, None, :]
    return jnp.where(receivers == hottest, CAP, base_count).astype(jnp.int32)


def with_ends(result, key, least, top_value):
    longest = result.shape.index(max(result.shape))
    spots = []
    for shift in (0, 1):
        where = [jax.random.randint(jax.random.fold_in(key, axis), (), 0, length) for axis, length in enumerate(result.shape)]
        where[longest] = (where[longest] + shift) % result.shape[longest]
        spots.append(tuple(where))
    return result.at[spots[0]].set(least).at[spots[1]].set(top_value)


def level_of(rng, dims, pieces, least, largest):
    def one(position, shards_of):
        draws = jax.random.uniform(jax.random.fold_in(jax.random.fold_in(rng, 6), position), (shards_of,), jnp.float32, least / len(pieces), largest / len(pieces))
        return jnp.repeat(jnp.exp(draws), dims[position] // shards_of).reshape((-1,) + (1,) * (len(dims) - position - 1))

    gain = one(*pieces[0])
    for cut in pieces[1:]:
        gain = gain * one(*cut)
    return gain


def normal_values(stream_key, dims, width, most, shards=(), kind=jnp.bfloat16):
    entries = width * jax.random.normal(stream_key, dims, jnp.float32)
    if shards:
        entries = entries * level_of(stream_key, dims, shards, -0.22, 0.18)
    return jnp.clip(entries, -most, most).astype(kind)


def setup_inputs(seed: int = 0) -> dict:
    splits = jax.random.split(jax.random.key(seed), 11)
    return {
        "point_feats": normal_values(splits[0], (SAMPLES, PBLOCKS, C, BP), 1.0, 6.0, ((0, 16), (1, 2))),
        "point_coords": jnp.clip(1.0 * jax.random.uniform(splits[1], (SAMPLES, PBLOCKS, 3, BP), jnp.float32) ** level_of(splits[1], (SAMPLES, PBLOCKS, 3, BP), ((0, 16), (1, 2)), -0.2, 0.2), 0.0, 1.0).astype(jnp.bfloat16),
        "slot_block": with_ends(jax.random.randint(splits[2], (SAMPLES, N_SLAB, N_SLAB, CAP), 0, PB_DEV), jax.random.fold_in(splits[2], 1), 0, PB_DEV - 1).astype(jnp.int32),
        "slot_cell": draw_slot_cell(jax.random.fold_in(splits[10], 71), 0),
        "slot_count": draw_slot_count(jax.random.fold_in(splits[10], 71), 0),
        "cotangent": normal_values(splits[5], (SAMPLES, KM, KM, KM, 2 * C), 1.0, 6.0, ((0, 16), (1, 2)), jnp.float32),
        "offset_map": normal_values(splits[6], (KH, 3), 3.0, 12.0, (), jnp.float32),
        "offset_bias": normal_values(splits[7], (KH,), 1.0, 4.0, (), jnp.float32),
        "kernel_mix": normal_values(splits[8], (KH, C, C), C ** -0.5, 0.75),
        "lift_weight": normal_values(splits[9], (C, C), C ** -0.5, 0.75),
    }


def slot_kernel(mixed_feats, coords, cell_x, cell_y, offset_map, offset_bias):
    pos_z = (jnp.arange(GZ).astype(jnp.float32) + 0.5) / GZ
    pos_x = (cell_x.astype(jnp.float32) + 0.5) / GX
    pos_y = (cell_y.astype(jnp.float32) + 0.5) / GY
    coef_x = offset_map[:, 0][:, None]
    coef_y = offset_map[:, 1][:, None]
    coef_z = offset_map[:, 2][:, None]
    cell_part = coef_x * pos_x + coef_y * pos_y + coef_z * pos_z[None, :]
    points_f = coords.astype(jnp.float32)
    point_part = coef_x * points_f[0][None, :] + coef_y * points_f[1][None, :] + coef_z * points_f[2][None, :]
    weights = jax.nn.relu(cell_part[:, :, None] - point_part[:, None, :] + offset_bias[:, None, None]).astype(jnp.bfloat16)
    flat_weights = jnp.transpose(weights, (1, 0, 2)).reshape(GZ, KH * BP)
    slot_sum = jnp.dot(flat_weights, mixed_feats.reshape(KH * BP, C), preferred_element_type=jnp.float32) * (1.0 / BP)
    return slot_sum.reshape(GZ * C)

def spectral_modes(slot_terms, cell_ids, cell_x, cell_y, lift_weight, spec_scale):
    slot_total = cell_ids.shape[0]
    is_live = cell_ids >= 0
    same_cell = (cell_ids[:, None] == cell_ids[None, :]) & is_live[None, :]
    slot_index = jnp.arange(slot_total, dtype=jnp.int32)
    before = same_cell & (slot_index[None, :] < slot_index[:, None])
    leader = (is_live & jnp.logical_not(jnp.any(before, axis=1))).astype(jnp.float32)
    summed = jnp.dot(same_cell.astype(jnp.float32), slot_terms, precision=lax.Precision.HIGHEST, preferred_element_type=jnp.float32)
    latent = summed.astype(jnp.bfloat16).reshape(slot_total * GZ, C)
    lifted = jax.nn.gelu(jnp.dot(latent, lift_weight, preferred_element_type=jnp.float32)).reshape(slot_total, GZ, C)
    lifted = lifted * leader[:, None, None]
    cells_z = jnp.arange(GZ, dtype=jnp.int32)
    mode_freq = jnp.arange(KM, dtype=jnp.int32)
    z_turn = jnp.mod(cells_z[:, None] * mode_freq[None, :], GZ).astype(jnp.float32) * (2.0 * math.pi / GZ)
    z_table = jnp.concatenate([jnp.cos(z_turn), -jnp.sin(z_turn)], axis=1)
    z_modes = jnp.einsum('nzc,zk->nkc', lifted, z_table, precision=lax.Precision.HIGHEST, preferred_element_type=jnp.float32)
    real_z = z_modes[:, :KM].reshape(slot_total, KM * C)
    imag_z = z_modes[:, KM:].reshape(slot_total, KM * C)
    signed = jnp.where(mode_freq < KM // 2, mode_freq, mode_freq - KM)
    step_x = jnp.mod(cell_x[:, None].astype(jnp.int32) * signed[None, :], GX).astype(jnp.float32)
    step_y = jnp.mod(cell_y[:, None].astype(jnp.int32) * signed[None, :], GY).astype(jnp.float32)
    phase_angle = (step_x[:, :, None] / GX + step_y[:, None, :] / GY) * (2.0 * math.pi)
    phase_angle = phase_angle.reshape(slot_total, KM * KM)
    cos_part = jnp.cos(phase_angle)
    sin_part = -jnp.sin(phase_angle)
    contract = (((0,), (0,)), ((), ()))
    high = lax.Precision.HIGHEST
    real_x = lax.dot_general(cos_part, real_z, contract, precision=high, preferred_element_type=jnp.float32) - lax.dot_general(sin_part, imag_z, contract, precision=high, preferred_element_type=jnp.float32)
    imag_x = lax.dot_general(cos_part, imag_z, contract, precision=high, preferred_element_type=jnp.float32) + lax.dot_general(sin_part, real_z, contract, precision=high, preferred_element_type=jnp.float32)
    out_shape = (KM, KM, KM, C)
    return jnp.concatenate([real_x.reshape(out_shape), imag_x.reshape(out_shape)], axis=3) * spec_scale

def sample_modes(feats, coords, blocks, cells, counts, offset_map, offset_bias, kernel_mix, lift_weight):
    planes = GX // N_SLAB
    mixed_all = jnp.einsum('ncp,hcd->nhpd', feats.astype(jnp.float32), kernel_mix.astype(jnp.float32), precision=lax.Precision.HIGHEST).astype(jnp.bfloat16)
    src_index = jnp.arange(N_SLAB, dtype=jnp.int32)[:, None, None]
    dst_index = jnp.arange(N_SLAB, dtype=jnp.int32)[None, :, None]
    slot_order = jnp.arange(CAP, dtype=jnp.int32)[None, None, :]
    is_live = slot_order < counts[:, :, None]
    block_ids = (src_index * PB_DEV + blocks).reshape(-1).astype(jnp.int32)
    cell_x = (dst_index * planes + cells // GY).reshape(-1).astype(jnp.int32)
    cell_y = (cells % GY).reshape(-1).astype(jnp.int32)
    cell_ids = jnp.where(is_live, dst_index * (planes * GY) + cells, -1).reshape(-1).astype(jnp.int32)

    def one_slot(slot_args):
        block_id, row_x, row_y = slot_args
        return slot_kernel(mixed_all[block_id], coords[block_id], row_x, row_y, offset_map, offset_bias)
    slot_terms = lax.map(one_slot, (block_ids, cell_x, cell_y))
    spec_scale = 1.0 / math.sqrt(GZ * N_SLAB * N_SLAB * CAP)
    return spectral_modes(slot_terms, cell_ids, cell_x, cell_y, lift_weight, spec_scale)

def reference(point_feats, point_coords, slot_block, slot_cell, slot_count, cotangent, offset_map, offset_bias, kernel_mix, lift_weight):

    def per_sample(sample_args):
        feats, coords, blocks, cells, counts = sample_args
        return sample_modes(feats, coords, blocks, cells, counts, offset_map, offset_bias, kernel_mix, lift_weight)
    all_modes = lax.map(per_sample, (point_feats, point_coords, slot_block, slot_cell, slot_count))
    real_modes = all_modes[..., :C]
    imag_modes = all_modes[..., C:]
    grad_real = cotangent[..., :C]
    grad_imag = cotangent[..., C:]
    left_side = jnp.concatenate([grad_real, grad_imag], axis=4)
    right_side = jnp.concatenate([grad_imag, -grad_real], axis=4)
    high = lax.Precision.HIGHEST
    first_sum = jnp.einsum('bxyzi,bxyzo->ixyzo', real_modes, left_side, precision=high)
    second_sum = jnp.einsum('bxyzi,bxyzo->ixyzo', imag_modes, right_side, precision=high)
    return first_sum + second_sum
```

```python
import functools
import math

import jax
import jax.numpy as jnp
from jax import lax
from jax.experimental import pallas as pl
from jax.experimental.pallas import tpu as pltpu
from jax.sharding import PartitionSpec as P

GX = 128
GY = 128
GZ = 128
VMEM_LIMIT = 48 * 1024 * 1024
HIGH = lax.Precision.HIGHEST
ROWS0 = (((0,), (0,)), ((), ()))


def slot_kernel(
    peer_ref, block_ref, cell_ref, count_ref, zcoef_ref, feats_ref, coords_ref, map_ref,
    bias_ref, mix_ref, out_ref, acc_ref, part_ref, turned_ref,
):
    peer = peer_ref[0]
    capacity = block_ref.shape[1]
    hidden, channels = mix_ref.shape[0], mix_ref.shape[1]
    points = feats_ref.shape[2]
    planes = peer_ref[1]
    width = capacity * channels
    tags = []
    for j in range(capacity):
        block = block_ref[peer, j]
        cell = cell_ref[peer, j]
        row_x = peer * planes + lax.div(cell, GY)
        row_y = lax.rem(cell, GY)
        pos_x = (row_x.astype(jnp.float32) + 0.5) * (1.0 / GX)
        pos_y = (row_y.astype(jnp.float32) + 0.5) * (1.0 / GY)
        spots = coords_ref[block].astype(jnp.float32)
        point_part = (
            map_ref[:, 0:1] * spots[0:1, :]
            + map_ref[:, 1:2] * spots[1:2, :]
            + map_ref[:, 2:3] * spots[2:3, :]
        )
        shift = map_ref[:, 0:1] * pos_x + map_ref[:, 1:2] * pos_y + bias_ref[...]
        part_ref[j] = shift - point_part
        turned_ref[:, j * channels : (j + 1) * channels] = (
            feats_ref[block].astype(jnp.float32).T.astype(jnp.bfloat16)
        )
        tags.append(jnp.where(j < count_ref[peer], cell, -1).astype(jnp.float32))
    acc_ref[...] = jnp.zeros_like(acc_ref)
    pos_z = (lax.broadcasted_iota(jnp.int32, (GZ, points), 0).astype(jnp.float32) + 0.5) * (
        1.0 / GZ
    )
    diag = (
        lax.broadcasted_iota(jnp.int32, (width, width), 0) // channels
        == lax.broadcasted_iota(jnp.int32, (width, width), 1) // channels
    )
    step = 4

    def body(it, carry):
        mixed, weights = [], []
        for u in range(step):
            h = it * step + u
            mix = mix_ref[h]
            wide = jnp.concatenate([mix] * capacity, axis=1)
            tall = jnp.concatenate([wide] * capacity, axis=0)
            spread = jnp.where(diag, tall, jnp.zeros_like(tall))
            mixed.append(
                jnp.dot(turned_ref[...], spread, preferred_element_type=jnp.float32).astype(
                    jnp.bfloat16
                )
            )
            cell_z = pos_z * zcoef_ref[h]
            rows = [
                jnp.maximum(cell_z + part_ref[j, pl.ds(h, 1), :], 0.0).astype(jnp.bfloat16)
                for j in range(capacity)
            ]
            weights.append(jnp.concatenate(rows, axis=0))
        acc_ref[...] += jnp.dot(
            jnp.concatenate(weights, axis=1),
            jnp.concatenate(mixed, axis=0),
            preferred_element_type=jnp.float32,
        )
        return carry

    lax.fori_loop(0, hidden // step, body, 0)
    for j in range(capacity):
        terms = acc_ref[j * GZ : (j + 1) * GZ, j * channels : (j + 1) * channels]
        out_ref[j * channels : (j + 1) * channels, :] = terms.T * (1.0 / points)
    row = lax.broadcasted_iota(jnp.int32, (8, GZ), 0)
    tag_rows = jnp.full((8, GZ), -1.0, jnp.float32)
    for j in range(capacity):
        tag_rows = jnp.where(row == j, tags[j], tag_rows)
    out_ref[capacity * channels :, :] = tag_rows


def slot_terms(peer_info, slot_block, slot_cell, slot_count, zcoef, feats, coords, offset_map,
               offset_bias, kernel_mix):
    capacity = slot_block.shape[1]
    channels, points = feats.shape[1], feats.shape[2]
    hidden = kernel_mix.shape[0]
    smem = pl.BlockSpec(memory_space=pltpu.SMEM)
    vmem = pl.BlockSpec(memory_space=pltpu.VMEM)
    width = capacity * channels
    return pl.pallas_call(
        slot_kernel,
        out_shape=jax.ShapeDtypeStruct((width + 8, GZ), jnp.float32),
        in_specs=[smem] * 5 + [vmem] * 5,
        out_specs=vmem,
        scratch_shapes=[
            pltpu.VMEM((capacity * GZ, width), jnp.float32),
            pltpu.VMEM((capacity, hidden, points), jnp.float32),
            pltpu.VMEM((points, width), jnp.bfloat16),
        ],
        compiler_params=pltpu.CompilerParams(vmem_limit_bytes=VMEM_LIMIT),
        cost_estimate=pl.CostEstimate(
            flops=2 * capacity * GZ * hidden * points * width, bytes_accessed=2 << 20,
            transcendentals=0,
        ),
        name="slot_terms",
    )(peer_info, slot_block, slot_cell, slot_count, zcoef, feats, coords, offset_map, offset_bias,
      kernel_mix)


def lift_kernel(groups, capacity, dests, copies, *refs):
    terms = refs[:groups]
    lift_ref, table_ref, out_ref, tag_ref, wide_ref = refs[groups:]
    channels = lift_ref.shape[0]
    kept = channels // dests
    slots = groups * capacity
    lanes = out_ref.shape[1]
    per = 2 * slots

    def tag_of(m):
        base = capacity * channels + m % capacity
        return terms[m // capacity][base : base + 1, :]

    def terms_of(m):
        base = (m % capacity) * channels
        return terms[m // capacity][base : base + channels, :]

    for n in range(slots):
        tag = tag_of(n)
        live = tag >= 0.0
        summed = jnp.zeros((channels, GZ), jnp.float32)
        leader = live
        for m in range(slots):
            same = (tag_of(m) == tag) & live
            summed = summed + jnp.where(same, terms_of(m), 0.0)
            if m < n:
                leader = leader & jnp.logical_not(same)
        latent = summed.astype(jnp.bfloat16)
        lifted = jax.nn.gelu(
            jnp.dot(lift_ref[...], latent, preferred_element_type=jnp.float32)
        )
        lifted = jnp.where(leader, lifted, 0.0)
        for i in range(kept):
            wide_ref[n * dests : (n + 1) * dests, i * GZ : (i + 1) * GZ] = lifted[
                i * dests : (i + 1) * dests, :
            ]
        tag_ref[n : n + 1, :] = tag
    modes = jnp.dot(
        wide_ref[...], table_ref[...], precision=HIGH, preferred_element_type=jnp.float32
    )
    tags = tag_ref[:, :lanes]
    for n in range(slots):
        piece = modes[n * dests : (n + 1) * dests, :]
        for t in range(copies):
            out_ref[pl.ds(t * per + n, dests, stride=copies * per), :] = piece
    for d in range(dests * copies):
        out_ref[d * per + slots : (d + 1) * per, :] = tags


def lift_slots(terms, lift_rows, table, capacity, dests, copies):
    groups = len(terms)
    channels = lift_rows.shape[0]
    slots = groups * capacity
    lanes = table.shape[1]
    vmem = pl.BlockSpec(memory_space=pltpu.VMEM)
    return pl.pallas_call(
        functools.partial(lift_kernel, groups, capacity, dests, copies),
        out_shape=jax.ShapeDtypeStruct((dests * copies * 2 * slots, lanes), jnp.float32),
        in_specs=[vmem] * (groups + 2),
        out_specs=vmem,
        scratch_shapes=[
            pltpu.VMEM((slots, GZ), jnp.float32),
            pltpu.VMEM((slots * dests, channels // dests * GZ), jnp.float32),
        ],
        compiler_params=pltpu.CompilerParams(vmem_limit_bytes=VMEM_LIMIT),
        cost_estimate=pl.CostEstimate(
            flops=1 << 27, bytes_accessed=1 << 20, transcendentals=1 << 16
        ),
        name="lift_slots",
    )(*terms, lift_rows, table)


def modes_kernel(samples, slabs, slots, planes, scale, group, order_ref, recv_ref, freq_ref,
                 out_ref, all_ref):
    lanes = recv_ref.shape[1]
    total = freq_ref.shape[1]
    half = lanes // 2
    per = 2 * slots

    def body(q, carry):
        sample = order_ref[q]
        waves, values = [], []
        for t in range(slabs):
            base = pl.multiple_of((sample * slabs + t) * per, 8)
            piece = recv_ref[pl.ds(base, slots), :]
            tag = jnp.maximum(recv_ref[pl.ds(base + slots, slots), :][:, 0:1], 0.0)
            local_x = jnp.floor(tag * (1.0 / GY))
            turns = (local_x + t * planes) * (1.0 / GX) * freq_ref[0:1, :] + (
                tag - local_x * GY
            ) * (1.0 / GY) * freq_ref[1:2, :]
            values.append(piece)
            waves.append((turns - jnp.floor(turns)) * (2.0 * math.pi))
        angle = jnp.concatenate(waves, axis=0)
        plain = jnp.concatenate(values, axis=0)
        crossed = jnp.concatenate([plain[:, half:], -plain[:, :half]], axis=1)
        modes = lax.dot_general(
            jnp.concatenate([jnp.cos(angle), jnp.sin(angle)], axis=0),
            jnp.concatenate([plain, crossed], axis=0),
            ROWS0,
            precision=HIGH,
            preferred_element_type=jnp.float32,
        )
        all_ref[pl.ds(q, total, stride=samples), :] = modes * scale
        return carry

    lax.fori_loop(0, samples, body, 0)
    span = group * samples
    for block in range(total // group):
        out_ref[block] = all_ref[block * span : (block + 1) * span, :].T.astype(jnp.bfloat16)


def sample_modes(order, recv, freqs, samples, slabs, slots, planes, scale, group):
    lanes = recv.shape[1]
    total = freqs.shape[1]
    vmem = pl.BlockSpec(memory_space=pltpu.VMEM)
    return pl.pallas_call(
        functools.partial(modes_kernel, samples, slabs, slots, planes, scale, group),
        out_shape=jax.ShapeDtypeStruct((total // group, lanes, group * samples), jnp.bfloat16),
        in_specs=[pl.BlockSpec(memory_space=pltpu.SMEM), vmem, vmem],
        out_specs=vmem,
        scratch_shapes=[pltpu.VMEM((total * samples, lanes), jnp.float32)],
        compiler_params=pltpu.CompilerParams(vmem_limit_bytes=VMEM_LIMIT),
        cost_estimate=pl.CostEstimate(
            flops=1 << 27, bytes_accessed=1 << 20, transcendentals=1 << 16
        ),
        name="sample_modes",
    )(order, recv, freqs)


def grad_kernel(samples, group, depth, aliased, *refs):
    modes_ref, pick_ref, mask_ref = refs[:3]
    rows_refs = refs[3 : 3 + samples]
    out_ref = refs[3 + samples + aliased]
    lanes = modes_ref.shape[1]
    half_rows = lanes // 2
    kept = out_ref.shape[0]
    half = out_ref.shape[2] // 2
    span = samples * depth
    block = modes_ref[0]
    for g in range(group):
        left = jnp.dot(
            block, pick_ref[:, g * span : (g + 1) * span], preferred_element_type=jnp.float32
        )
        left = (left * mask_ref[...]).astype(jnp.bfloat16)
        right = jnp.concatenate([r[g * depth : (g + 1) * depth, :] for r in rows_refs], axis=0)
        both = jnp.dot(left, right, preferred_element_type=jnp.float32)
        plain, turned = both[:half_rows], both[half_rows:]
        total = plain + jnp.concatenate([turned[:, half:], -turned[:, :half]], axis=1)
        for i in range(kept):
            out_ref[i, g * depth : (g + 1) * depth, :] = total[i * depth : (i + 1) * depth]


def grad_chunk(modes, pick, mask, rows, kept, group, depth, chunk, chunks, previous):
    samples = len(rows)
    lanes = modes.shape[1]
    chunk_rows, width = rows[0].shape
    tile = group * depth
    steps = chunk_rows // tile
    in_specs = [
        pl.BlockSpec((1, lanes, group * samples), lambda s: (chunk * steps + s, 0, 0)),
        pl.BlockSpec(pick.shape, lambda s: (0, 0)),
        pl.BlockSpec(mask.shape, lambda s: (0, 0)),
    ] + [pl.BlockSpec((tile, width), lambda s: (s, 0))] * samples
    operands = [modes, pick, mask, *rows]
    aliases = {}
    if previous is not None:
        in_specs.append(pl.BlockSpec(memory_space=pl.ANY))
        aliases = {len(operands): 0}
        operands.append(previous)
    return pl.pallas_call(
        functools.partial(grad_kernel, samples, group, depth, int(previous is not None)),
        out_shape=jax.ShapeDtypeStruct((kept, chunk_rows * chunks, width), jnp.float32),
        grid=(steps,),
        in_specs=in_specs,
        out_specs=pl.BlockSpec((kept, tile, width), lambda s: (0, chunk * steps + s, 0)),
        input_output_aliases=aliases,
        compiler_params=pltpu.CompilerParams(vmem_limit_bytes=VMEM_LIMIT),
        cost_estimate=pl.CostEstimate(
            flops=2 * chunk_rows * lanes * samples * width * 2,
            bytes_accessed=chunk_rows * width * (2 * samples + 4 * kept),
            transcendentals=0,
        ),
        name="grad_chunk",
    )(*operands)


def chip_ring(chips):
    order = list(range(0, chips, 2))
    return order + [c for c in range(chips - 1, 0, -1) if c % 2]


def ring_perm(chips, step):
    order = chip_ring(chips)
    return [
        (2 * order[p] + core, 2 * order[(p + step) % chips] + core)
        for p in range(chips)
        for core in (0, 1)
    ]


def gather_chunk(rows, devices, forward):
    chips = devices // 2
    swap = [(d, d ^ 1) for d in range(devices)]
    half = chips // 2
    ahead = half if forward else chips - 1 - half
    chain = {0: rows}
    up = down = rows
    for s in range(1, max(ahead, chips - 1 - ahead) + 1):
        if s <= ahead:
            up = lax.ppermute(up, "dp", ring_perm(chips, 1))
            chain[s] = up
        if s <= chips - 1 - ahead:
            down = lax.ppermute(down, "dp", ring_perm(chips, -1))
            chain[chips - s] = down
    result = []
    for s in range(chips):
        result += [chain[s], lax.ppermute(chain[s], "dp", swap)]
    return result


def ring_order(devices):
    chips = devices // 2
    order = chip_ring(chips)
    place = [order.index(c) for c in range(chips)]
    table = []
    for d in range(devices):
        chip, core = d // 2, d % 2
        row = []
        for s in range(chips):
            source = order[(place[chip] - s) % chips]
            row += [2 * source + core, 2 * source + 1 - core]
        table.append(row)
    return jnp.array(table, jnp.int32)


def per_device(
    point_feats, point_coords, slot_block, slot_cell, slot_count, cotangent, offset_map,
    offset_bias, kernel_mix, lift_weight,
):
    slabs = lax.axis_size("slab")
    devices = lax.axis_size("dp")
    slab_index = lax.axis_index("slab")
    channels = point_feats.shape[2]
    mode_count = cotangent.shape[2]
    capacity = slot_block.shape[3]
    width = cotangent.shape[4]
    planes = GX // slabs
    kept = channels // devices
    lanes = 2 * kept * mode_count
    slots = slabs * capacity
    local_x = cotangent.shape[1]
    total = local_x * mode_count
    chunks = 2
    group = min(8, total // chunks)

    rows = cotangent[0].reshape(-1, width).astype(jnp.bfloat16)
    size = rows.shape[0] // chunks
    gathered = [
        gather_chunk(rows[c * size : (c + 1) * size], devices, c % 2 == 0) for c in range(chunks)
    ]

    terms = []
    for s in list(range(1, slabs)) + [0]:
        peer = lax.rem(slab_index + s, slabs)
        part = slot_terms(
            jnp.stack([peer, jnp.int32(planes)]), slot_block[0, 0], slot_cell[0, 0],
            slot_count[0, 0], offset_map[:, 2], point_feats[0], point_coords[0], offset_map,
            offset_bias[:, None], kernel_mix,
        )
        if s:
            part = lax.ppermute(part, "slab", [(t, (t + s) % slabs) for t in range(slabs)])
        terms.append(part)

    cells_z = jnp.arange(GZ, dtype=jnp.int32)
    mode_freq = jnp.arange(mode_count, dtype=jnp.int32)
    z_turn = jnp.mod(cells_z[:, None] * mode_freq[None, :], GZ).astype(jnp.float32) * (
        2.0 * math.pi / GZ
    )
    z_table = jnp.stack([jnp.cos(z_turn), -jnp.sin(z_turn)], axis=1)
    table = (
        jnp.eye(kept, dtype=jnp.float32)[:, None, None, :, None] * z_table[None, :, :, None, :]
    ).reshape(kept * GZ, lanes)
    lift_rows = lift_weight.T.reshape(devices, kept, channels).swapaxes(0, 1).reshape(
        channels, channels
    )
    payload = lift_slots(terms, lift_rows, table, capacity, devices, slabs)
    recv = lax.all_to_all(
        payload.reshape(devices * slabs, 2 * slots, lanes), ("dp", "slab"), split_axis=0,
        concat_axis=0, tiled=True,
    ).reshape(payload.shape)

    signed = jnp.where(mode_freq < mode_count // 2, mode_freq, mode_freq - mode_count)
    grid_x = lax.dynamic_slice_in_dim(signed, slab_index * local_x, local_x)
    freqs = jnp.stack(
        [jnp.repeat(grid_x, mode_count), jnp.tile(signed, local_x)]
    ).astype(jnp.float32)
    order = ring_order(devices)[lax.axis_index("dp")]
    scale = 1.0 / math.sqrt(GZ * slabs * slabs * capacity)
    modes = sample_modes(order, recv, freqs, devices, slabs, slots, planes, scale, group)

    span = devices * mode_count
    pick_row = jnp.arange(group * devices, dtype=jnp.int32)[:, None]
    pick_col = jnp.arange(group * span, dtype=jnp.int32)[None, :]
    pick = (pick_row == pick_col // mode_count).astype(jnp.bfloat16)
    mask = (
        jnp.arange(lanes, dtype=jnp.int32)[:, None] % mode_count
        == jnp.arange(span, dtype=jnp.int32)[None, :] % mode_count
    ).astype(jnp.float32)
    result = None
    for c in range(chunks):
        result = grad_chunk(
            modes, pick, mask, gathered[c], kept, group, mode_count, c, chunks, result
        )
    return result.reshape(kept, local_x, mode_count, mode_count, width)


def solution(mesh):
    placed = (
        P("dp", "slab", None, None),
        P("dp", "slab", None, None),
        P("dp", "slab", None, None),
        P("dp", "slab", None, None),
        P("dp", "slab", None),
        P("dp", "slab", None, None, None),
        P(),
        P(),
        P(),
        P(),
    )
    return jax.shard_map(
        per_device,
        mesh=mesh,
        in_specs=placed,
        out_specs=P("dp", "slab", None, None, None),
        check_vma=False,
    )
```

```python
import functools
import math

import jax
import jax.numpy as jnp
from jax import lax
from jax.experimental import pallas as pl
from jax.experimental.pallas import tpu as pltpu
from jax.sharding import PartitionSpec as P

GX = 128
GY = 128
GZ = 128
MIB = 1024 * 1024


def in_hbm(*arrays):
    return [pltpu.with_memory_space_constraint(a, pltpu.HBM) for a in arrays]


def work(micros):
    return pl.CostEstimate(flops=int(micros * 10**9), bytes_accessed=1024, transcendentals=0)


HIGH = lax.Precision.HIGHEST
ROWS0 = (((0,), (0,)), ((), ()))


def slot_kernel(slabs, planes, block_hbm, cell_hbm, count_hbm, feats_hbm, coords_hbm, map_hbm, bias_hbm, mix_hbm, after_hbm, *refs):
    del after_hbm
    outs = refs[:slabs]
    (block_ref, cell_ref, count_ref, feats_ref, coords_ref, map_ref, bias_ref, mix_ref, list_ref,
     turned_ref, mixed_ref, part_ref, coef_ref, flat_ref, acc_ref, spot_ref, sems) = refs[slabs:]
    me = lax.axis_index("slab")
    pairs = [(block_hbm, block_ref), (cell_hbm, cell_ref), (count_hbm, count_ref), (feats_hbm, feats_ref),
             (coords_hbm, coords_ref), (map_hbm, map_ref), (bias_hbm, bias_ref), (mix_hbm, mix_ref)]
    copies = [pltpu.make_async_copy(a, b, sems.at[i]) for i, (a, b) in enumerate(pairs)]
    for c in copies: c.start()
    capacity = block_ref.shape[1]
    blocks, channels, points = feats_ref.shape
    hidden = mix_ref.shape[0]
    width = blocks * channels
    base = capacity * channels + 8
    row8 = lax.broadcasted_iota(jnp.int32, (8, points), 0)
    pos_z = (lax.broadcasted_iota(jnp.int32, (GZ, points), 0).astype(jnp.float32) + 0.5) * (1.0 / GZ)
    for c in copies[:7]: c.wait()
    spot_ref[...] = coords_ref[...].astype(jnp.float32)
    for b in range(blocks):
        turned_ref[:, b * channels : (b + 1) * channels] = feats_ref[b].astype(jnp.float32).T.astype(jnp.bfloat16)
    cat = jnp.concatenate([map_ref[...], bias_ref[...], jnp.zeros((4, hidden), jnp.float32)], axis=0)
    coef_ref[...] = lax.dot_general(cat, jnp.where(row8 == 2, 1.0, 0.0), ROWS0, precision=HIGH, preferred_element_type=jnp.float32)
    live = jnp.int32(0)
    for r in range(slabs):
        peer = lax.rem(me + r, slabs)
        tag_rows = jnp.full((8, points), -1.0, jnp.float32)
        for j in range(capacity):
            n = r * capacity + j
            block = block_ref[peer, j]
            cell = cell_ref[peer, j]
            alive = j < count_ref[peer]
            @pl.when(alive)
            def _():
                list_ref[live] = n
                list_ref[live + 1] = n
            live = live + alive.astype(jnp.int32)
            list_ref[slabs * capacity + 1 + n] = block
            pos_x = ((peer * planes + lax.div(cell, GY)).astype(jnp.float32) + 0.5) * (1.0 / GX)
            pos_y = (lax.rem(cell, GY).astype(jnp.float32) + 0.5) * (1.0 / GY)
            q0 = spot_ref[0, pl.ds(block, 1), :]
            q1 = spot_ref[1, pl.ds(block, 1), :]
            q2 = spot_ref[2, pl.ds(block, 1), :]
            side = jnp.where(row8 == 0, pos_x - q0, jnp.where(row8 == 1, pos_y - q1, jnp.where(row8 == 2, -q2, jnp.where(row8 == 3, 1.0, 0.0))))
            part_ref[n] = lax.dot_general(cat, side, ROWS0, precision=HIGH, preferred_element_type=jnp.float32)
            tag_rows = jnp.where(row8 == j, jnp.where(alive, cell, -1).astype(jnp.float32), tag_rows)
        flat_ref[r * base + capacity * channels : (r + 1) * base, :] = tag_rows
    copies[7].wait()
    lane = lax.broadcasted_iota(jnp.int32, (channels, 2 * channels), 1)
    left = turned_ref[...]

    step = max(1, min(hidden // 2, 512 // (blocks * blocks)))

    def mix_step(it, carry):
        for u in range(step):
            h = it * step + u
            mix = mix_ref[h]
            wide = jnp.concatenate([mix, mix], axis=1)
            zero = jnp.zeros_like(wide)
            halves = (jnp.where(lane < channels, wide, zero), jnp.where(lane < channels, zero, wide))
            rows = [jnp.concatenate([halves[b % 2] if b // 2 == t else zero for t in range(blocks // 2)], axis=1) for b in range(blocks)]
            mixed_ref[pl.ds(pl.multiple_of(h * points, points), points), :] = jnp.dot(left, jnp.concatenate(rows, axis=0), preferred_element_type=jnp.float32).astype(jnp.bfloat16)
        return carry
    lax.fori_loop(0, hidden // step, mix_step, 0)

    def pair(it, carry):
        ids = [list_ref[2 * it], list_ref[2 * it + 1]]
        part = 8
        for k in range(0, hidden, part):
            cols = []
            for h in range(k, k + part):
                cell_z = pos_z * coef_ref[h : h + 1, :]
                cols.append(jnp.concatenate([jnp.maximum(cell_z + part_ref[n, h : h + 1, :], 0.0).astype(jnp.bfloat16) for n in ids], axis=0))
            got = jnp.dot(jnp.concatenate(cols, axis=1), mixed_ref[k * points : (k + part) * points, :], preferred_element_type=jnp.float32)
            if k: acc_ref[...] += got
            else: acc_ref[...] = got
        for j, n in enumerate(ids):
            block = list_ref[slabs * capacity + 1 + n]
            pick = acc_ref[j * GZ : (j + 1) * GZ, : 2 * channels]
            for t in range(1, blocks // 2):
                pick = jnp.where(block // 2 == t, acc_ref[j * GZ : (j + 1) * GZ, 2 * t * channels : 2 * (t + 1) * channels], pick)
            turned = pick.T * (1.0 / points)
            start = pl.multiple_of((n // capacity) * base + (n % capacity) * channels, 8)
            flat_ref[pl.ds(start, channels), :] = jnp.where(block % 2 == 1, turned[channels:], turned[:channels])
        return carry
    lax.fori_loop(0, (live + 1) // 2, pair, 0)
    for r in range(slabs):
        outs[r][...] = flat_ref[r * base : (r + 1) * base, :]

def slot_terms(slot_block, slot_cell, slot_count, feats, coords, offset_map, offset_bias, kernel_mix, planes, after):
    slabs, capacity = slot_block.shape
    blocks, channels, points = feats.shape
    hidden = kernel_mix.shape[0]
    base = capacity * channels + 8
    slots = slabs * capacity
    width = blocks * channels
    slot_limit = hidden * points * width * 2 + 16 * MIB
    hbm = pl.BlockSpec(memory_space=pltpu.HBM)
    vmem = pl.BlockSpec(memory_space=pltpu.VMEM)
    return pl.pallas_call(
        functools.partial(slot_kernel, slabs, planes),
        out_shape=[jax.ShapeDtypeStruct((base, GZ), jnp.float32)] * slabs,
        in_specs=[hbm] * 8 + [pl.BlockSpec(memory_space=pl.ANY)],
        out_specs=[vmem] * slabs,
        scratch_shapes=[
            pltpu.SMEM((slabs, capacity), jnp.int32), pltpu.SMEM((slabs, capacity), jnp.int32), pltpu.SMEM((slabs,), jnp.int32),
            pltpu.VMEM(feats.shape, feats.dtype), pltpu.VMEM(coords.shape, coords.dtype), pltpu.VMEM(offset_map.shape, jnp.float32),
            pltpu.VMEM(offset_bias.shape, jnp.float32), pltpu.VMEM(kernel_mix.shape, kernel_mix.dtype),
            pltpu.SMEM((2 * slots + 2,), jnp.int32),
            pltpu.VMEM((points, width), jnp.bfloat16), pltpu.VMEM((hidden * points, width), jnp.bfloat16),
            pltpu.VMEM((slots, hidden, points), jnp.float32), pltpu.VMEM((hidden, points), jnp.float32),
            pltpu.VMEM((slabs * base, GZ), jnp.float32), pltpu.VMEM((2 * GZ, width), jnp.float32), pltpu.VMEM(coords.shape, jnp.float32),
            pltpu.SemaphoreType.DMA((8,)),
        ],
        compiler_params=pltpu.CompilerParams(vmem_limit_bytes=slot_limit),
        cost_estimate=work(1),
        name="slot_terms",
    )(*in_hbm(slot_block, slot_cell, slot_count, feats, coords, offset_map, offset_bias, kernel_mix),
      after)


def lift_kernel(groups, capacity, dests, copies, mode_count, *refs):
    terms = refs[:groups]
    lift_ref, out_ref, tag_ref, row_ref, wide_ref, table_ref = refs[groups:]
    channels = lift_ref.shape[0]
    kept = channels // dests
    slots = groups * capacity
    lanes = table_ref.shape[1]
    tiles = lanes // GZ
    per = (tiles + 1) * slots
    cells = lax.broadcasted_iota(jnp.int32, (GZ, lanes), 0)
    lane = lax.broadcasted_iota(jnp.int32, (GZ, lanes), 1)
    step = cells * (lane % mode_count) + jnp.where(lane >= lanes // 2, GZ // 4, 0)
    waves = jnp.cos((step % GZ).astype(jnp.float32) * (2.0 * math.pi / GZ))
    for i in range(kept):
        mine = lane // mode_count % kept == i
        table_ref[i * GZ : (i + 1) * GZ, :] = jnp.where(mine, waves, 0.0)

    def tag_of(m):
        base = capacity * channels + m % capacity
        return terms[m // capacity][base : base + 1, :]

    def terms_of(m):
        base = (m % capacity) * channels
        return terms[m // capacity][base : base + channels, :]

    for n in range(slots):
        tag = tag_of(n)
        live = tag >= 0.0
        summed = jnp.zeros((channels, GZ), jnp.float32)
        leader = live
        for m in range(slots):
            same = (tag_of(m) == tag) & live
            summed = summed + jnp.where(same, terms_of(m), 0.0)
            if m < n:
                leader = leader & jnp.logical_not(same)
        latent = summed.astype(jnp.bfloat16)
        lifted = jax.nn.gelu(
            lax.dot_general(lift_ref[...], latent, ROWS0, preferred_element_type=jnp.float32)
        )
        row_ref[n] = jnp.where(leader, lifted, 0.0)
        for i in range(kept):
            wide_ref[n * dests : (n + 1) * dests, i * GZ : (i + 1) * GZ] = row_ref[
                n, pl.ds(i, dests, stride=kept), :
            ]
        tag_ref[n : n + 1, :] = tag
    modes = jnp.dot(
        wide_ref[...], table_ref[...], precision=HIGH, preferred_element_type=jnp.float32
    )
    for n in range(slots):
        piece = modes[n * dests : (n + 1) * dests, :]
        for t in range(copies):
            for u in range(tiles):
                out_ref[pl.ds(t * per + u * slots + n, dests, stride=copies * per), :] = piece[
                    :, u * GZ : (u + 1) * GZ
                ]
    for d in range(dests * copies):
        out_ref[d * per + tiles * slots : (d + 1) * per, :] = tag_ref[...]


def lift_slots(terms, lift_weight, capacity, dests, copies, mode_count):
    groups = len(terms)
    channels = lift_weight.shape[0]
    slots = groups * capacity
    kept = channels // dests
    lanes = 2 * kept * mode_count
    vmem = pl.BlockSpec(memory_space=pltpu.VMEM)
    return pl.pallas_call(
        functools.partial(lift_kernel, groups, capacity, dests, copies, mode_count),
        out_shape=jax.ShapeDtypeStruct((dests * copies * (lanes // GZ + 1) * slots, GZ), jnp.float32),
        in_specs=[vmem] * (groups + 1),
        out_specs=vmem,
        scratch_shapes=[
            pltpu.VMEM((slots, GZ), jnp.float32),
            pltpu.VMEM((slots, channels, GZ), jnp.float32),
            pltpu.VMEM((slots * dests, kept * GZ), jnp.float32),
            pltpu.VMEM((kept * GZ, lanes), jnp.float32),
        ],
        compiler_params=pltpu.CompilerParams(vmem_limit_bytes=16 * MIB),
        cost_estimate=work(0.1),
        name="lift_slots",
    )(*terms, lift_weight)


def modes_kernel(samples, slabs, slots, planes, scale, group, mode_count, recv_ref, out_ref,
                 all_ref):
    tiles = all_ref.shape[0]
    total = all_ref.shape[1] // samples
    half = tiles * GZ // 2
    per = (tiles + 1) * slots
    device = lax.axis_index("dp")
    first_x = (lax.axis_index("slab") * 2 + lax.rem(device, 2)) * (total // mode_count)
    spot = lax.broadcasted_iota(jnp.int32, (1, total), 1)
    freq_x = first_x + spot // mode_count
    freq_y = spot % mode_count
    freq_x = jnp.where(freq_x < mode_count // 2, freq_x, freq_x - mode_count).astype(jnp.float32)
    freq_y = jnp.where(freq_y < mode_count // 2, freq_y, freq_y - mode_count).astype(jnp.float32)

    def body(q, carry):
        sample = ring_sample(device, q, samples)
        waves, values = [], []
        for t in range(slabs):
            base = pl.multiple_of((sample * slabs + t) * per, 8)
            piece = jnp.concatenate(
                [recv_ref[pl.ds(base + u * slots, slots), :] for u in range(tiles)], axis=1
            )
            tag = jnp.maximum(recv_ref[pl.ds(base + tiles * slots, slots), :][:, 0:1], 0.0)
            local_x = jnp.floor(tag * (1.0 / GY))
            turns = (local_x + t * planes) * (1.0 / GX) * freq_x + (
                tag - local_x * GY
            ) * (1.0 / GY) * freq_y
            values.append(piece)
            waves.append((turns - jnp.floor(turns)) * (2.0 * math.pi))
        angle = jnp.concatenate(waves, axis=0)
        plain = jnp.concatenate(values, axis=0)
        crossed = jnp.concatenate([plain[:, half:], -plain[:, :half]], axis=1)
        modes = lax.dot_general(
            jnp.concatenate([jnp.cos(angle), jnp.sin(angle)], axis=0),
            jnp.concatenate([plain, crossed], axis=0),
            ROWS0,
            precision=HIGH,
            preferred_element_type=jnp.float32,
        )
        for u in range(tiles):
            all_ref[u, pl.ds(q, total, stride=samples), :] = (
                modes[:, u * GZ : (u + 1) * GZ] * scale
            )
        return carry

    lax.fori_loop(0, samples, body, 0, unroll=4)
    span = group * samples
    for block in range(total // group):
        for u in range(tiles):
            out_ref[block, u * GZ : (u + 1) * GZ, :] = all_ref[
                u, block * span : (block + 1) * span, :
            ].T.astype(jnp.bfloat16)


def sample_modes(recv, samples, slabs, slots, planes, scale, group, total, mode_count, lanes):
    vmem = pl.BlockSpec(memory_space=pltpu.VMEM)
    return pl.pallas_call(
        functools.partial(
            modes_kernel, samples, slabs, slots, planes, scale, group, mode_count
        ),
        out_shape=jax.ShapeDtypeStruct((total // group, lanes, group * samples), jnp.bfloat16),
        in_specs=[vmem],
        out_specs=vmem,
        scratch_shapes=[pltpu.VMEM((lanes // GZ, total * samples, GZ), jnp.float32)],
        compiler_params=pltpu.CompilerParams(vmem_limit_bytes=16 * MIB),
        cost_estimate=work(0.2),
        name="sample_modes",
    )(recv)


def grad_kernel(samples, group, depth, aliased, core_ref, modes_ref, *refs):
    rows_refs = refs[:samples]
    own_ref, other_ref, pick_ref, mask_ref = refs[samples + aliased :]
    lanes = modes_ref.shape[1]
    half_rows = lanes // 2
    kept = own_ref.shape[0]
    half = own_ref.shape[2] // 2
    span = samples * depth
    first = core_ref[0] == 0

    @pl.when(pl.program_id(0) == 0)
    def _():
        row = lax.broadcasted_iota(jnp.int32, pick_ref.shape, 0)
        col = lax.broadcasted_iota(jnp.int32, pick_ref.shape, 1)
        pick_ref[...] = jnp.where(row == col // depth, 1.0, 0.0).astype(jnp.bfloat16)
        row = lax.broadcasted_iota(jnp.int32, mask_ref.shape, 0)
        col = lax.broadcasted_iota(jnp.int32, mask_ref.shape, 1)
        mask_ref[...] = jnp.where(row % depth == col % depth, 1.0, 0.0)

    lefts = []
    for block in range(modes_ref.shape[0]):
        modes = modes_ref[block]
        for g in range(group):
            left = jnp.dot(
                modes, pick_ref[:, g * span : (g + 1) * span], preferred_element_type=jnp.float32
            )
            lefts.append((left * mask_ref[...]).astype(jnp.bfloat16))
    for g, left in enumerate(lefts):
        spot = slice(g * depth, (g + 1) * depth)
        right = jnp.concatenate([r[spot, :] for r in rows_refs], axis=0)
        both = jnp.dot(left, right, preferred_element_type=jnp.float32)
        plain, turned = both[:half_rows], both[half_rows:]
        total = plain + jnp.concatenate([turned[:, half:], -turned[:, :half]], axis=1)
        low, high = total[: half_rows // 2], total[half_rows // 2 :]
        own, other = jnp.where(first, low, high), jnp.where(first, high, low)
        for i in range(kept):
            own_ref[i, spot, :] = own[i * depth : (i + 1) * depth]
            other_ref[i, spot, :] = other[i * depth : (i + 1) * depth]


def grad_chunk(core, modes, rows, kept, group, depth, chunk, chunks, previous):
    samples = len(rows)
    lanes = modes.shape[1]
    total_rows, width = rows[0].shape
    size = total_rows // chunks
    blocks = min(2, size // (group * depth))
    tile = blocks * group * depth
    steps = size // tile
    in_specs = [
        pl.BlockSpec((blocks, lanes, group * samples), lambda s, c: (chunk * steps + s, 0, 0)),
    ]
    in_specs += [pl.BlockSpec((tile, width), lambda s, c: (chunk * steps + s, 0))] * samples
    operands = [modes, *rows]
    aliases = {}
    if previous is not None:
        in_specs.append(pl.BlockSpec(memory_space=pl.ANY))
        aliases = {1 + len(operands): 0}
        operands.append(previous)
    return pl.pallas_call(
        functools.partial(grad_kernel, samples, group, depth, int(previous is not None)),
        out_shape=[
            jax.ShapeDtypeStruct((kept, 2 * total_rows, width), jnp.float32),
            jax.ShapeDtypeStruct((kept, size, width), jnp.float32),
        ],
        grid_spec=pltpu.PrefetchScalarGridSpec(
            num_scalar_prefetch=1,
            grid=(steps,),
            in_specs=in_specs,
            out_specs=[
                pl.BlockSpec(
                    (kept, tile, width), lambda s, c: (0, (c[0] * chunks + chunk) * steps + s, 0)
                ),
                pl.BlockSpec((kept, tile, width), lambda s, c: (0, s, 0)),
            ],
            scratch_shapes=[
                pltpu.VMEM((group * samples, group * samples * depth), jnp.bfloat16),
                pltpu.VMEM((lanes, samples * depth), jnp.float32),
            ],
        ),
        input_output_aliases=aliases,
        compiler_params=pltpu.CompilerParams(vmem_limit_bytes=24 * MIB),
        cost_estimate=work(1),
        name="grad_chunk",
    )(core, *operands)


def place_kernel(core_ref, part_ref, old_ref, out_ref):
    del core_ref, old_ref
    out_ref[...] = part_ref[...]


def place_chunk(core, part, result, chunk, chunks):
    kept, size, width = part.shape
    steps = 2
    tile = size // steps
    return pl.pallas_call(
        place_kernel,
        out_shape=jax.ShapeDtypeStruct(result.shape, result.dtype),
        grid_spec=pltpu.PrefetchScalarGridSpec(
            num_scalar_prefetch=1,
            grid=(steps,),
            in_specs=[
                pl.BlockSpec((kept, tile, width), lambda s, c: (0, s, 0)),
                pl.BlockSpec(memory_space=pl.ANY),
            ],
            out_specs=pl.BlockSpec(
                (kept, tile, width),
                lambda s, c: (0, ((1 - c[0]) * chunks + chunk) * steps + s, 0),
            ),
        ),
        input_output_aliases={2: 0},
        compiler_params=pltpu.CompilerParams(vmem_limit_bytes=8 * MIB),
        cost_estimate=work(0.2),
        name="place_chunk",
    )(core, part, result)


def cast_kernel(parts, rows_hbm, keep_ref, give_ref, held_ref, sems):
    size = held_ref.shape[0] // (2 * parts)
    core = lax.rem(lax.axis_index("dp"), 2)
    halves = [(keep_ref, core * parts), (give_ref, (1 - core) * parts)]
    copies, jobs = [], []
    for h, (out, first) in enumerate(halves):
        for i in range(parts):
            source = pl.ds(pl.multiple_of((first + i) * size, size), size)
            spot = pl.ds((h * parts + i) * size, size)
            copies.append(
                pltpu.make_async_copy(
                    rows_hbm.at[source, :], held_ref.at[spot, :], sems.at[h * parts + i]
                )
            )
            jobs.append((out, pl.ds(i * size, size), spot))
    for copy in copies:
        copy.start()
    for copy, (out, place, spot) in zip(copies, jobs):
        copy.wait()
        out[place, :] = held_ref[spot, :].astype(jnp.bfloat16)


def cast_rows(rows):
    parts = 2
    total, width = rows.shape
    return pl.pallas_call(
        functools.partial(cast_kernel, parts),
        out_shape=[jax.ShapeDtypeStruct((total // 2, width), jnp.bfloat16)] * 2,
        in_specs=[pl.BlockSpec(memory_space=pltpu.HBM)],
        out_specs=[pl.BlockSpec(memory_space=pltpu.VMEM)] * 2,
        scratch_shapes=[
            pltpu.VMEM(rows.shape, jnp.float32),
            pltpu.SemaphoreType.DMA((2 * parts,)),
        ],
        compiler_params=pltpu.CompilerParams(vmem_limit_bytes=8 * MIB),
        cost_estimate=work(0.1),
        name="cast_rows",
    )(*in_hbm(rows))


def chip_ring(chips):
    order = list(range(0, chips, 2))
    return order + [c for c in range(chips - 1, 0, -1) if c % 2]


def ring_perm(chips, step):
    order = chip_ring(chips)
    return [
        (2 * order[p] + core, 2 * order[(p + step) % chips] + core)
        for p in range(chips)
        for core in (0, 1)
    ]


def ring_sample(device, q, devices):
    chips = devices // 2
    up = (chips + 1) // 2
    chip = lax.div(device, 2)
    place = jnp.where(lax.rem(chip, 2) == 0, lax.div(chip, 2), chips - 1 - lax.div(chip, 2))
    spot = lax.rem(place - lax.div(q, 2) + chips, chips)
    source = jnp.where(spot < up, 2 * spot, 2 * (chips - 1 - spot) + 1)
    return 2 * source + lax.rem(lax.rem(device, 2) + lax.rem(q, 2), 2)


def joint_kernel(count, total, *refs):
    for old, new in zip(refs[:count], refs[total:]):
        new[...] = old[...]


def joint(arrays, *after):
    vmem = pl.BlockSpec(memory_space=pltpu.VMEM)
    total = len(arrays) + len(after)
    return pl.pallas_call(
        functools.partial(joint_kernel, len(arrays), total),
        out_shape=[jax.ShapeDtypeStruct(a.shape, a.dtype) for a in arrays],
        in_specs=[vmem] * total,
        out_specs=[vmem] * len(arrays),
        compiler_params=pltpu.CompilerParams(vmem_limit_bytes=8 * MIB),
        cost_estimate=work(0.01),
        name="joint",
    )(*arrays, *after)


def per_device(
    point_feats, point_coords, slot_block, slot_cell, slot_count, cotangent, offset_map,
    offset_bias, kernel_mix, lift_weight,
):
    slabs = lax.axis_size("slab")
    devices = lax.axis_size("dp")
    channels = point_feats.shape[2]
    mode_count = cotangent.shape[2]
    capacity = slot_block.shape[3]
    width = cotangent.shape[4]
    planes = GX // slabs
    kept = channels // devices
    slots = slabs * capacity
    local_x = cotangent.shape[1]
    total = local_x // 2 * mode_count
    chunks = 2
    group = min(8, total // chunks)
    chips = devices // 2
    far = chips // 2

    def up(rows):
        return lax.ppermute(rows, "dp", ring_perm(chips, 1))

    def down(rows):
        return lax.ppermute(rows, "dp", ring_perm(chips, -1))

    def swap(rows):
        return lax.ppermute(rows, "dp", [(d, d ^ 1) for d in range(devices)])

    own, twin = {}, {}
    own[0], given = cast_rows(cotangent[0].reshape(-1, width))
    own[1], own[chips - 1] = up(own[0]), down(own[0])
    twin[0] = swap(given)
    twin[1], twin[chips - 1] = up(twin[0]), down(twin[0])
    terms = list(slot_terms(
        slot_block[0, 0], slot_cell[0, 0], slot_count[0, 0], point_feats[0],
        jnp.swapaxes(point_coords[0], 0, 1), offset_map.T, offset_bias[None], kernel_mix, planes,
        twin[0],
    ))
    own[1], own[chips - 1], *terms = joint([own[1], own[chips - 1], *terms])
    own[2], own[chips - 2] = up(own[1]), down(own[chips - 1])
    for s in range(1, slabs):
        terms[s] = lax.ppermute(terms[s], "slab", [(t, (t + s) % slabs) for t in range(slabs)])
    twin[1], twin[chips - 1], *terms = joint([twin[1], twin[chips - 1], *terms], own[1])
    twin[2], twin[chips - 2] = up(twin[1]), down(twin[chips - 1])
    payload = lift_slots(terms, lift_weight, capacity, chips, 2 * slabs, mode_count)
    own[2], own[chips - 2], payload = joint([own[2], own[chips - 2], payload], twin[1])
    recv = lax.all_to_all(
        payload.reshape(devices * slabs, -1, GZ), ("dp", "slab"),
        split_axis=0, concat_axis=0, tiled=True,
    ).reshape(payload.shape)
    own[3], own[chips - 3] = up(own[2]), down(own[chips - 2])
    twin[2], twin[chips - 2] = joint([twin[2], twin[chips - 2]], own[2])
    scale = 1.0 / math.sqrt(GZ * slabs * slabs * capacity)
    modes = sample_modes(
        recv, devices, slabs, slots, planes, scale, group, total, mode_count, 4 * kept * mode_count
    )
    twin[3], twin[chips - 3] = up(twin[2]), down(twin[chips - 2])
    for s in range(4, far):
        own[s], own[chips - s] = up(own[s - 1]), down(own[chips - s + 1])
        twin[s], twin[chips - s] = up(twin[s - 1]), down(twin[chips - s + 1])
    own[far - 1], own[far + 1] = joint([own[far - 1], own[far + 1]], twin[2])
    twin[far - 1], twin[far + 1] = joint([twin[far - 1], twin[far + 1]], own[far - 1])
    own[far], twin[far] = up(own[far - 1]), down(twin[far + 1])

    rows = [r for p in range(chips) for r in (own[p], twin[p])]
    core = lax.rem(lax.axis_index("dp"), 2).reshape(1)
    result, parts = None, []
    for c in range(chunks):
        result, part = grad_chunk(core, modes, rows, kept, group, mode_count, c, chunks, result)
        parts.append(swap(part))
    for c, part in enumerate(parts):
        result = place_chunk(core, part, result, c, chunks)
    return result.reshape(kept, local_x, mode_count, mode_count, width)


def solution(mesh):
    placed = (
        P("dp", "slab", None, None),
        P("dp", "slab", None, None),
        P("dp", "slab", None, None),
        P("dp", "slab", None, None),
        P("dp", "slab", None),
        P("dp", "slab", None, None, None),
        P(),
        P(),
        P(),
        P(),
    )
    return jax.shard_map(
        per_device,
        mesh=mesh,
        in_specs=placed,
        out_specs=P("dp", "slab", None, None, None),
        check_vma=False,
    )
```

```python
import functools
import math

import jax
import jax.numpy as jnp
from jax import lax
from jax.experimental import pallas as pl
from jax.experimental.pallas import tpu as pltpu
from jax.sharding import PartitionSpec as P

GX = 128
GY = 128
GZ = 128
MIB = 1024 * 1024


def in_hbm(*arrays):
    return [pltpu.with_memory_space_constraint(a, pltpu.HBM) for a in arrays]


def work(micros):
    return pl.CostEstimate(flops=int(micros * 10**9), bytes_accessed=1024, transcendentals=0)


HIGH = lax.Precision.HIGHEST
ROWS0 = (((0,), (0,)), ((), ()))


def slot_kernel(slabs, planes, block_hbm, cell_hbm, count_hbm, feats_hbm, coords_hbm, map_hbm, bias_hbm, mix_hbm, after_hbm, *refs):
    del after_hbm
    outs = refs[:2]
    (block_ref, cell_ref, count_ref, feats_ref, coords_ref, map_ref, bias_ref, mix_ref, list_ref,
     turned_ref, mixed_ref, part_ref, coef_ref, out_ref, acc_ref, spot_ref, sems) = refs[2:]
    me = lax.axis_index("slab")
    pairs = [(block_hbm, block_ref), (cell_hbm, cell_ref), (count_hbm, count_ref), (feats_hbm, feats_ref),
             (coords_hbm, coords_ref), (map_hbm, map_ref), (bias_hbm, bias_ref), (mix_hbm, mix_ref)]
    copies = [pltpu.make_async_copy(a, b, sems.at[i]) for i, (a, b) in enumerate(pairs)]
    for c in copies: c.start()
    capacity = block_ref.shape[1]
    blocks, channels, points = feats_ref.shape
    hidden = mix_ref.shape[0]
    width = blocks * channels
    base = capacity * channels + 8
    row8 = lax.broadcasted_iota(jnp.int32, (8, points), 0)
    pos_z = (lax.broadcasted_iota(jnp.int32, (GZ, points), 0).astype(jnp.float32) + 0.5) * (1.0 / GZ)
    for c in copies[:7]: c.wait()
    spot_ref[...] = coords_ref[...].astype(jnp.float32)
    for b in range(blocks):
        turned_ref[:, b * channels : (b + 1) * channels] = feats_ref[b].astype(jnp.float32).T.astype(jnp.bfloat16)
    cat = jnp.concatenate([map_ref[...], bias_ref[...], jnp.zeros((4, hidden), jnp.float32)], axis=0)
    live = jnp.int32(0)
    sides = [jnp.where(row8 == 2, 1.0, 0.0)]
    for r in range(slabs):
        peer = lax.rem(me + r, slabs)
        tag_rows = jnp.full((8, points), -1.0, jnp.float32)
        for j in range(capacity):
            n = r * capacity + j
            block = block_ref[peer, j]
            cell = cell_ref[peer, j]
            alive = j < count_ref[peer]
            @pl.when(alive)
            def _():
                list_ref[live] = n
                list_ref[live + 1] = n
            live = live + alive.astype(jnp.int32)
            list_ref[slabs * capacity + 1 + n] = block
            pos_x = ((peer * planes + lax.div(cell, GY)).astype(jnp.float32) + 0.5) * (1.0 / GX)
            pos_y = (lax.rem(cell, GY).astype(jnp.float32) + 0.5) * (1.0 / GY)
            q0 = spot_ref[0, pl.ds(block, 1), :]
            q1 = spot_ref[1, pl.ds(block, 1), :]
            q2 = spot_ref[2, pl.ds(block, 1), :]
            side = jnp.where(row8 == 0, pos_x - q0, jnp.where(row8 == 1, pos_y - q1, jnp.where(row8 == 2, -q2, jnp.where(row8 == 3, 1.0, 0.0))))
            sides.append(side)
            tag_rows = jnp.where(row8 == j, jnp.where(alive, cell, -1).astype(jnp.float32), tag_rows)
        out_ref[r * base + capacity * channels : (r + 1) * base, :] = tag_rows
    parts = lax.dot_general(
        cat, jnp.concatenate(sides, axis=1), ROWS0, precision=HIGH,
        preferred_element_type=jnp.float32,
    )
    coef_ref[...] = parts[:, :points]
    for n in range(slabs * capacity):
        part_ref[n] = parts[:, (n + 1) * points : (n + 2) * points]
    copies[7].wait()
    lane = lax.broadcasted_iota(jnp.int32, (channels, 2 * channels), 1)
    left = turned_ref[...]

    step = max(1, min(hidden // 2, 512 // (blocks * blocks)))

    def mix_step(it, carry):
        for u in range(step):
            h = it * step + u
            mix = mix_ref[h]
            wide = jnp.concatenate([mix, mix], axis=1)
            zero = jnp.zeros_like(wide)
            halves = (jnp.where(lane < channels, wide, zero), jnp.where(lane < channels, zero, wide))
            rows = [jnp.concatenate([halves[b % 2] if b // 2 == t else zero for t in range(blocks // 2)], axis=1) for b in range(blocks)]
            mixed_ref[pl.ds(pl.multiple_of(h * points, points), points), :] = jnp.dot(left, jnp.concatenate(rows, axis=0), preferred_element_type=jnp.float32).astype(jnp.bfloat16)
        return carry
    lax.fori_loop(0, hidden // step, mix_step, 0)

    def pair(it, carry):
        ids = [list_ref[2 * it], list_ref[2 * it + 1]]
        part = 8
        for k in range(0, hidden, part):
            cols = []
            for h in range(k, k + part):
                cell_z = pos_z * coef_ref[h : h + 1, :]
                cols.append(jnp.concatenate([jnp.maximum(cell_z + part_ref[n, h : h + 1, :], 0.0).astype(jnp.bfloat16) for n in ids], axis=0))
            got = jnp.dot(jnp.concatenate(cols, axis=1), mixed_ref[k * points : (k + part) * points, :], preferred_element_type=jnp.float32)
            if k: acc_ref[...] += got
            else: acc_ref[...] = got
        for j, n in enumerate(ids):
            block = list_ref[slabs * capacity + 1 + n]
            pick = acc_ref[j * GZ : (j + 1) * GZ, : 2 * channels]
            for t in range(1, blocks // 2):
                pick = jnp.where(block // 2 == t, acc_ref[j * GZ : (j + 1) * GZ, 2 * t * channels : 2 * (t + 1) * channels], pick)
            turned = pick.T * (1.0 / points)
            start = pl.multiple_of((n // capacity) * base + (n % capacity) * channels, 8)
            out_ref[pl.ds(start, channels), :] = jnp.where(block % 2 == 1, turned[channels:], turned[:channels])
        return carry
    lax.fori_loop(0, (live + 1) // 2, pair, 0)
    for i, out in enumerate(outs):
        out[...] = out_ref[i * out.shape[0] : (i + 1) * out.shape[0], :]

def slot_terms(slot_block, slot_cell, slot_count, feats, coords, offset_map, offset_bias, kernel_mix, planes, after):
    slabs, capacity = slot_block.shape
    blocks, channels, points = feats.shape
    hidden = kernel_mix.shape[0]
    base = capacity * channels + 8
    slots = slabs * capacity
    width = blocks * channels
    slot_limit = hidden * points * width * 2 + (10 if blocks <= 4 else 24) * MIB
    hbm = pl.BlockSpec(memory_space=pltpu.HBM)
    vmem = pl.BlockSpec(memory_space=pltpu.VMEM)
    return pl.pallas_call(
        functools.partial(slot_kernel, slabs, planes),
        out_shape=[jax.ShapeDtypeStruct((slabs * base // 2, GZ), jnp.float32)] * 2,
        in_specs=[hbm] * 8 + [pl.BlockSpec(memory_space=pl.ANY)],
        out_specs=[vmem] * 2,
        scratch_shapes=[
            pltpu.SMEM((slabs, capacity), jnp.int32), pltpu.SMEM((slabs, capacity), jnp.int32), pltpu.SMEM((slabs,), jnp.int32),
            pltpu.VMEM(feats.shape, feats.dtype), pltpu.VMEM(coords.shape, coords.dtype), pltpu.VMEM(offset_map.shape, jnp.float32),
            pltpu.VMEM(offset_bias.shape, jnp.float32), pltpu.VMEM(kernel_mix.shape, kernel_mix.dtype),
            pltpu.SMEM((2 * slots + 2,), jnp.int32),
            pltpu.VMEM((points, width), jnp.bfloat16), pltpu.VMEM((hidden * points, width), jnp.bfloat16),
            pltpu.VMEM((slots, hidden, points), jnp.float32), pltpu.VMEM((hidden, points), jnp.float32),
            pltpu.VMEM((slabs * base, GZ), jnp.float32), pltpu.VMEM((2 * GZ, width), jnp.float32), pltpu.VMEM(coords.shape, jnp.float32),
            pltpu.SemaphoreType.DMA((8,)),
        ],
        compiler_params=pltpu.CompilerParams(vmem_limit_bytes=slot_limit),
        cost_estimate=work(1),
        name="slot_terms",
    )(*in_hbm(slot_block, slot_cell, slot_count, feats, coords, offset_map, offset_bias, kernel_mix),
      after)


def lift_kernel(slabs, capacity, dests, mode_count, *refs):
    terms = refs[:slabs]
    lift_ref, out_ref, tag_ref, row_ref, wide_ref, table_ref = refs[slabs:]
    channels = lift_ref.shape[0]
    kept = channels // dests
    group = slabs * capacity
    slots = slabs * group
    base = capacity * channels + 8
    lanes = table_ref.shape[1]
    tiles = lanes // GZ
    per = out_ref.shape[0] // dests
    cells = lax.broadcasted_iota(jnp.int32, (GZ, lanes), 0)
    lane = lax.broadcasted_iota(jnp.int32, (GZ, lanes), 1)
    step = cells * (lane % mode_count) + jnp.where(lane >= lanes // 2, GZ // 4, 0)
    waves = jnp.cos((step % GZ).astype(jnp.float32) * (2.0 * math.pi / GZ))
    for i in range(kept):
        mine = lane // mode_count % kept == i
        table_ref[i * GZ : (i + 1) * GZ, :] = jnp.where(mine, waves, 0.0)

    def receiver(u, carry):
        starts = [lax.rem(u + s, slabs) * base for s in range(slabs)]

        def tag_of(m):
            first = pl.multiple_of(starts[m // capacity] + capacity * channels, 8)
            return terms[m // capacity][pl.ds(first, 8), :][m % capacity : m % capacity + 1, :]

        def terms_of(m):
            first = pl.multiple_of(starts[m // capacity] + (m % capacity) * channels, 8)
            return terms[m // capacity][pl.ds(first, channels), :]

        tags = [tag_of(m) for m in range(group)]
        for n in range(group):
            live = tags[n] >= 0.0
            summed = jnp.zeros((channels, GZ), jnp.float32)
            leader = live
            for m in range(group):
                same = (tags[m] == tags[n]) & live
                summed = summed + jnp.where(same, terms_of(m), 0.0)
                if m < n:
                    leader = leader & jnp.logical_not(same)
            latent = summed.astype(jnp.bfloat16)
            lifted = jax.nn.gelu(
                lax.dot_general(lift_ref[...], latent, ROWS0, preferred_element_type=jnp.float32)
            )
            row_ref[n] = jnp.where(leader, lifted, 0.0)
            rows = pl.ds(pl.multiple_of((u * group + n) * dests, 8), dests)
            for i in range(kept):
                wide_ref[rows, i * GZ : (i + 1) * GZ] = row_ref[
                    n, pl.ds(i, dests, stride=kept), :
                ]
        tag_ref[pl.ds(pl.multiple_of(u * group, 8), group), :] = jnp.concatenate(tags, axis=0)
        return carry

    lax.fori_loop(0, slabs, receiver, 0, unroll=slabs <= 2)
    modes = jnp.dot(
        wide_ref[...], table_ref[...], precision=HIGH, preferred_element_type=jnp.float32
    )
    for n in range(slots):
        for t in range(tiles):
            out_ref[pl.ds(t * slots + n, dests, stride=per), :] = modes[
                n * dests : (n + 1) * dests, t * GZ : (t + 1) * GZ
            ]
    row = lax.broadcasted_iota(jnp.int32, (slots, GZ), 0)
    lane = lax.broadcasted_iota(jnp.int32, (slots, GZ), 1)
    place = lax.broadcasted_iota(jnp.int32, (8, GZ), 0)
    packed = jnp.zeros((8, GZ), jnp.float32)
    for k in range((slots + GZ - 1) // GZ):
        line = jnp.sum(jnp.where(row == lane + k * GZ, tag_ref[...], 0.0), axis=0, keepdims=True)
        packed = jnp.where(place == k, line, packed)
    for d in range(dests):
        out_ref[d * per + tiles * slots : (d + 1) * per, :] = packed


def lift_slots(terms, lift_weight, capacity, dests, mode_count):
    slabs = len(terms)
    channels = lift_weight.shape[0]
    slots = slabs * slabs * capacity
    kept = channels // dests
    lanes = 2 * kept * mode_count
    per = lanes // GZ * slots + 8
    vmem = pl.BlockSpec(memory_space=pltpu.VMEM)
    return pl.pallas_call(
        functools.partial(lift_kernel, slabs, capacity, dests, mode_count),
        out_shape=jax.ShapeDtypeStruct((dests * per, GZ), jnp.float32),
        in_specs=[vmem] * (slabs + 1),
        out_specs=vmem,
        scratch_shapes=[
            pltpu.VMEM((slots, GZ), jnp.float32),
            pltpu.VMEM((slabs * capacity, channels, GZ), jnp.float32),
            pltpu.VMEM((slots * dests, kept * GZ), jnp.float32),
            pltpu.VMEM((kept * GZ, lanes), jnp.float32),
        ],
        compiler_params=pltpu.CompilerParams(
            vmem_limit_bytes=(8 if slabs <= 2 else 48) * MIB
        ),
        cost_estimate=work(0.1),
        name="lift_slots",
    )(*terms, lift_weight)


def modes_kernel(chips, slabs, slots, planes, scale, group, mode_count, *refs):
    recv_refs = refs[:2]
    out_ref, all_ref = refs[2:]
    samples = 2 * chips
    tiles = all_ref.shape[0]
    total = all_ref.shape[1] // samples
    half = tiles * GZ // 2
    per = recv_refs[0].shape[0] // chips

    device = lax.axis_index("dp")
    slab = lax.axis_index("slab")
    first_x = (slab * 2 + lax.rem(device, 2)) * (total // mode_count)
    spot = lax.broadcasted_iota(jnp.int32, (1, total), 1)
    freq_x = first_x + spot // mode_count
    freq_y = spot % mode_count
    freq_x = jnp.where(freq_x < mode_count // 2, freq_x, freq_x - mode_count)
    freq_y = jnp.where(freq_y < mode_count // 2, freq_y, freq_y - mode_count)
    freq_x, freq_y = freq_x.astype(jnp.float32), freq_y.astype(jnp.float32)

    row = lax.broadcasted_iota(jnp.int32, (slots, GZ), 0)
    lane = lax.broadcasted_iota(jnp.int32, (slots, GZ), 1)
    peer = slab + lax.broadcasted_iota(jnp.int32, (slots, 1), 0) // (slots // slabs)
    plane = jnp.where(peer >= slabs, peer - slabs, peer).astype(jnp.float32) * planes

    def body(p, carry):
        base = pl.multiple_of(ring_chip(lax.div(device, 2), p, chips) * per, 8)
        for core, ref in enumerate(recv_refs):
            plain = jnp.concatenate(
                [ref[pl.ds(base + u * slots, slots), :] for u in range(tiles)], axis=1
            )
            packed = ref[pl.ds(base + tiles * slots, 8), :]
            tag = jnp.zeros((slots, 1), jnp.float32)
            for k in range((slots + GZ - 1) // GZ):
                tag = tag + jnp.sum(
                    jnp.where(row == lane + k * GZ, packed[k : k + 1, :], 0.0),
                    axis=1,
                    keepdims=True,
                )
            tag = jnp.maximum(tag, 0.0)
            local_x = jnp.floor(tag * (1.0 / GY))
            turns = (local_x + plane) * (1.0 / GX) * freq_x + (
                tag - local_x * GY
            ) * (1.0 / GY) * freq_y
            angle = (turns - jnp.floor(turns)) * (2.0 * math.pi)
            crossed = jnp.concatenate([plain[:, half:], -plain[:, :half]], axis=1)
            modes = lax.dot_general(
                jnp.concatenate([jnp.cos(angle), jnp.sin(angle)], axis=0),
                jnp.concatenate([plain, crossed], axis=0),
                ROWS0,
                precision=HIGH,
                preferred_element_type=jnp.float32,
            )
            for u in range(tiles):
                all_ref[u, pl.ds(2 * p + core, total, stride=samples), :] = (
                    modes[:, u * GZ : (u + 1) * GZ] * scale
                )
        return carry

    lax.fori_loop(0, chips, body, 0, unroll=2)

    span = group * samples
    for block in range(total // group):
        for u in range(tiles):
            out_ref[block, u * GZ : (u + 1) * GZ, :] = all_ref[
                u, block * span : (block + 1) * span, :
            ].T.astype(jnp.bfloat16)


def sample_modes(recv, chips, slabs, slots, planes, scale, group, total, mode_count, lanes):
    samples = 2 * chips
    vmem = pl.BlockSpec(memory_space=pltpu.VMEM)
    return pl.pallas_call(
        functools.partial(modes_kernel, chips, slabs, slots, planes, scale, group, mode_count),
        out_shape=jax.ShapeDtypeStruct((total // group, lanes, group * samples), jnp.bfloat16),
        in_specs=[vmem] * len(recv),
        out_specs=vmem,
        scratch_shapes=[pltpu.VMEM((lanes // GZ, total * samples, GZ), jnp.float32)],
        compiler_params=pltpu.CompilerParams(vmem_limit_bytes=(8 if slabs <= 2 else 32) * MIB),
        cost_estimate=work(0.2),
        name="sample_modes",
    )(*recv)


def spread_kernel(depth, modes_ref, after_ref, out_ref, pick_ref, mask_ref):
    del after_ref
    group = out_ref.shape[0]
    span = out_ref.shape[2]

    @pl.when(pl.program_id(0) == 0)
    def _():
        row = lax.broadcasted_iota(jnp.int32, pick_ref.shape, 0)
        col = lax.broadcasted_iota(jnp.int32, pick_ref.shape, 1)
        pick_ref[...] = jnp.where(row == col // depth, 1.0, 0.0).astype(jnp.bfloat16)
        row = lax.broadcasted_iota(jnp.int32, mask_ref.shape, 0)
        col = lax.broadcasted_iota(jnp.int32, mask_ref.shape, 1)
        mask_ref[...] = jnp.where(row % depth == col % depth, 1.0, 0.0)

    for g in range(group):
        left = jnp.dot(
            modes_ref[0], pick_ref[:, g * span : (g + 1) * span],
            preferred_element_type=jnp.float32,
        )
        out_ref[g] = (left * mask_ref[...]).astype(jnp.bfloat16)


def spread_modes(modes, group, depth, after):
    blocks, lanes, columns = modes.shape
    span = columns // group * depth
    return pl.pallas_call(
        functools.partial(spread_kernel, depth),
        out_shape=jax.ShapeDtypeStruct((blocks * group, lanes, span), jnp.bfloat16),
        grid=(blocks,),
        in_specs=[
            pl.BlockSpec((1, lanes, columns), lambda s: (s, 0, 0)),
            pl.BlockSpec(memory_space=pl.ANY),
        ],
        out_specs=pl.BlockSpec((group, lanes, span), lambda s: (s, 0, 0)),
        scratch_shapes=[
            pltpu.VMEM((columns, group * span), jnp.bfloat16),
            pltpu.VMEM((lanes, span), jnp.float32),
        ],
        compiler_params=pltpu.CompilerParams(vmem_limit_bytes=8 * MIB),
        cost_estimate=work(0.2),
        name="spread_modes",
    )(modes, after)


def grad_kernel(chunk, chunks, depth, firsts, aliased, modes_ref, *refs):
    samples = len(firsts)
    rows_refs = refs[:samples]
    out_hbm, other_ref, own_ref, sems = refs[samples + aliased :]
    half_rows = modes_ref.shape[1] // 2
    kept, size, width = other_ref.shape
    half = width // 2
    core = lax.rem(lax.axis_index("dp"), 2)
    first = core == 0
    group = min(16, size // depth)
    tile = group * depth
    steps = size // tile

    def write(s):
        start = pl.multiple_of(s * tile, tile)
        place = pl.multiple_of((core * chunks + chunk) * size + s * tile, tile)
        return pltpu.make_async_copy(
            own_ref.at[:, pl.ds(start, tile), :], out_hbm.at[:, pl.ds(place, tile), :], sems.at[s]
        )

    def body(s, carry):
        for g in range(group):
            start = pl.multiple_of(s * tile + g * depth, depth)
            right = jnp.concatenate(
                [r[pl.ds(at + start, depth), :] for r, at in zip(rows_refs, firsts)], axis=0
            )
            left = modes_ref[(chunk * steps + s) * group + g]
            both = jnp.dot(left, right, preferred_element_type=jnp.float32)
            plain, turned = both[:half_rows], both[half_rows:]
            total = plain + jnp.concatenate([turned[:, half:], -turned[:, :half]], axis=1)
            low, high = total[: half_rows // 2], total[half_rows // 2 :]
            own, other = jnp.where(first, low, high), jnp.where(first, high, low)
            for i in range(kept):
                own_ref[i, pl.ds(start, depth), :] = own[i * depth : (i + 1) * depth]
                other_ref[i, pl.ds(start, depth), :] = other[i * depth : (i + 1) * depth]
        write(s).start()
        return carry

    lax.fori_loop(0, steps, body, 0)
    for s in range(steps):
        write(s).wait()


def grad_chunk(modes, rows, kept, depth, chunk, chunks, previous):
    size, width = rows[0][0].shape[0] // chunks, rows[0][0].shape[1]
    hbm = pl.BlockSpec(memory_space=pl.ANY)
    vmem = pl.BlockSpec(memory_space=pltpu.VMEM)
    operands = [modes, *[array for array, _ in rows]]
    in_specs = [vmem] * len(operands)
    aliases = {}
    if previous is not None:
        in_specs.append(hbm)
        aliases = {len(operands): 0}
        operands.append(previous)
    steps = size // depth // min(16, size // depth)
    firsts = [first for _, first in rows]
    return pl.pallas_call(
        functools.partial(grad_kernel, chunk, chunks, depth, firsts, int(previous is not None)),
        out_shape=[
            jax.ShapeDtypeStruct((kept, 2 * chunks * size, width), jnp.float32),
            jax.ShapeDtypeStruct((kept, size, width), jnp.float32),
        ],
        in_specs=in_specs,
        out_specs=[hbm, vmem],
        scratch_shapes=[
            pltpu.VMEM((kept, size, width), jnp.float32),
            pltpu.SemaphoreType.DMA((steps,)),
        ],
        input_output_aliases=aliases,
        compiler_params=pltpu.CompilerParams(vmem_limit_bytes=24 * MIB),
        cost_estimate=work(1),
        name="grad_chunk",
    )(*operands)


def place_kernel(chunk, chunks, part_ref, old_hbm, out_hbm, sems):
    del old_hbm
    kept, size, _ = part_ref.shape
    core = lax.rem(lax.axis_index("dp"), 2)
    start = pl.multiple_of(((1 - core) * chunks + chunk) * size, size)
    copies = [
        pltpu.make_async_copy(part_ref.at[i], out_hbm.at[i, pl.ds(start, size), :], sems.at[i])
        for i in range(kept)
    ]
    for copy in copies:
        copy.start()
    for copy in copies:
        copy.wait()


def place_chunk(part, result, chunk, chunks):
    hbm = pl.BlockSpec(memory_space=pl.ANY)
    return pl.pallas_call(
        functools.partial(place_kernel, chunk, chunks),
        out_shape=jax.ShapeDtypeStruct(result.shape, result.dtype),
        in_specs=[pl.BlockSpec(memory_space=pltpu.VMEM), hbm],
        out_specs=hbm,
        scratch_shapes=[pltpu.SemaphoreType.DMA((part.shape[0],))],
        input_output_aliases={1: 0},
        compiler_params=pltpu.CompilerParams(vmem_limit_bytes=8 * MIB),
        cost_estimate=work(0.2),
        name="place_chunk",
    )(part, result)


def cast_kernel(parts, rows_hbm, keep_ref, give_ref, held_ref, sems):
    size = held_ref.shape[0] // (2 * parts)
    core = lax.rem(lax.axis_index("dp"), 2)
    halves = [(keep_ref, core * parts), (give_ref, (1 - core) * parts)]
    copies, jobs = [], []
    for h, (out, first) in enumerate(halves):
        for i in range(parts):
            source = pl.ds(pl.multiple_of((first + i) * size, size), size)
            spot = pl.ds((h * parts + i) * size, size)
            copies.append(
                pltpu.make_async_copy(
                    rows_hbm.at[source, :], held_ref.at[spot, :], sems.at[h * parts + i]
                )
            )
            jobs.append((out, pl.ds(i * size, size), spot))
    for copy in copies:
        copy.start()
    for copy, (out, place, spot) in zip(copies, jobs):
        copy.wait()
        out[place, :] = held_ref[spot, :].astype(jnp.bfloat16)


def cast_rows(rows):
    parts = 2
    total, width = rows.shape
    return pl.pallas_call(
        functools.partial(cast_kernel, parts),
        out_shape=[jax.ShapeDtypeStruct((total // 2, width), jnp.bfloat16)] * 2,
        in_specs=[pl.BlockSpec(memory_space=pltpu.HBM)],
        out_specs=[pl.BlockSpec(memory_space=pltpu.VMEM)] * 2,
        scratch_shapes=[
            pltpu.VMEM(rows.shape, jnp.float32),
            pltpu.SemaphoreType.DMA((2 * parts,)),
        ],
        compiler_params=pltpu.CompilerParams(vmem_limit_bytes=8 * MIB),
        cost_estimate=work(0.1),
        name="cast_rows",
    )(*in_hbm(rows))


def chip_ring(chips):
    order = list(range(0, chips, 2))
    return order + [c for c in range(chips - 1, 0, -1) if c % 2]


def ring_perm(chips, step):
    order = chip_ring(chips)
    return [
        (2 * order[p] + core, 2 * order[(p + step) % chips] + core)
        for p in range(chips)
        for core in (0, 1)
    ]


def ring_chip(chip, p, chips):
    up = (chips + 1) // 2
    place = jnp.where(lax.rem(chip, 2) == 0, lax.div(chip, 2), chips - 1 - lax.div(chip, 2))
    spot = lax.rem(place - p + chips, chips)
    return jnp.where(spot < up, 2 * spot, 2 * (chips - 1 - spot) + 1)


def joint_kernel(spans, total, *refs):
    for parts, new in zip(spans, refs[total:]):
        place = 0
        for source, start, size in parts:
            new[place : place + size] = refs[source][start : start + size]
            place += size


def joint(pieces, *after):
    arrays, spans = [], []

    def known(array):
        for i, other in enumerate(arrays):
            if other is array:
                return i
        arrays.append(array)
        return len(arrays) - 1

    for piece in pieces:
        parts = piece if isinstance(piece, list) else [piece]
        parts = [p if isinstance(p, tuple) else (p, 0, p.shape[0]) for p in parts]
        spans.append([(known(array), start, size) for array, start, size in parts])
    vmem = pl.BlockSpec(memory_space=pltpu.VMEM)
    operands = [*arrays, *after]
    return pl.pallas_call(
        functools.partial(joint_kernel, spans, len(operands)),
        out_shape=[
            jax.ShapeDtypeStruct(
                (sum(part[2] for part in parts), *arrays[parts[0][0]].shape[1:]),
                arrays[parts[0][0]].dtype,
            )
            for parts in spans
        ],
        in_specs=[vmem] * len(operands),
        out_specs=[vmem] * len(spans),
        compiler_params=pltpu.CompilerParams(vmem_limit_bytes=8 * MIB),
        cost_estimate=work(0.01),
        name="joint",
    )(*operands)


def per_device(
    point_feats, point_coords, slot_block, slot_cell, slot_count, cotangent, offset_map,
    offset_bias, kernel_mix, lift_weight,
):
    slabs = lax.axis_size("slab")
    devices = lax.axis_size("dp")
    channels = point_feats.shape[2]
    mode_count = cotangent.shape[2]
    capacity = slot_block.shape[3]
    width = cotangent.shape[4]
    planes = GX // slabs
    kept = channels // devices
    slots = slabs * slabs * capacity
    local_x = cotangent.shape[1]
    total = local_x // 2 * mode_count
    chunks = 2
    group = min(8, total // chunks)
    chips = devices // 2
    far = chips // 2

    def up(rows):
        return lax.ppermute(rows, "dp", ring_perm(chips, 1))

    def down(rows):
        return lax.ppermute(rows, "dp", ring_perm(chips, -1))

    def swap(rows):
        return lax.ppermute(rows, "dp", [(d, d ^ 1) for d in range(devices)])

    own, given = cast_rows(cotangent[0].reshape(-1, width))
    size = own.shape[0]
    ups, downs = [up(own)], [down(own)]
    twin = swap(given)
    ups.append(up(twin))
    downs.append(down(twin))

    sent = slot_terms(
        slot_block[0, 0], slot_cell[0, 0], slot_count[0, 0], point_feats[0],
        jnp.swapaxes(point_coords[0], 0, 1), offset_map.T, offset_bias[None], kernel_mix, planes,
        twin,
    )
    terms = [list(sent)] + [
        [lax.ppermute(x, "slab", [(t, (t + s) % slabs) for t in range(slabs)]) for x in sent]
        for s in range(1, slabs)
    ]
    held = {}
    held[1], held[chips - 1], *terms = joint([ups, downs, *terms])

    held[2], held[chips - 2] = up(held[1]), down(held[chips - 1])
    payload = lift_slots(terms, lift_weight, capacity, chips, mode_count)
    recv = lax.all_to_all(
        payload.reshape(chips, -1, GZ), "dp", split_axis=0, concat_axis=0, tiled=True,
        axis_index_groups=[list(range(c, devices, 2)) for c in range(2)],
    ).reshape(payload.shape)
    held[2], held[chips - 2], recv = joint([held[2], held[chips - 2], recv])

    for s in range(3, far):
        held[s], held[chips - s] = up(held[s - 1]), down(held[chips - s + 1])
    scale = 1.0 / math.sqrt(GZ * slabs * slabs * capacity)
    modes = sample_modes(
        [recv, swap(recv)], chips, slabs, slots, planes, scale, group, total, mode_count,
        4 * kept * mode_count,
    )
    half = size // 2
    held[far - 1], held[far + 1], first, second = joint(
        [
            held[far - 1],
            held[far + 1],
            [(held[far - 1], 0, half), (held[far - 1], size, half)],
            [(held[far + 1], half, half), (held[far + 1], size + half, half)],
        ],
        modes,
    )

    ends = [up(first), down(second)]
    modes = spread_modes(modes, group, mode_count, first)

    result, parts = None, []
    for c in range(chunks):
        rows = [(own, c * half), (twin, c * half)]
        for p in range(1, chips):
            if p == far:
                rows += [(ends[c], 0), (ends[c], half)]
            else:
                rows += [(held[p], c * half), (held[p], size + c * half)]
        result, part = grad_chunk(modes, rows, kept, mode_count, c, chunks, result)
        parts.append(swap(part))
    for c, part in enumerate(parts):
        result = place_chunk(part, result, c, chunks)
    return result.reshape(kept, local_x, mode_count, mode_count, width)


def solution(mesh):
    placed = (
        P("dp", "slab", None, None),
        P("dp", "slab", None, None),
        P("dp", "slab", None, None),
        P("dp", "slab", None, None),
        P("dp", "slab", None),
        P("dp", "slab", None, None, None),
        P(),
        P(),
        P(),
        P(),
    )
    return jax.shard_map(
        per_device,
        mesh=mesh,
        in_specs=placed,
        out_specs=P("dp", "slab", None, None, None),
        check_vma=False,
    )
```

```python
import functools
import math

import jax
import jax.numpy as jnp
from jax import lax
from jax.experimental import pallas as pl
from jax.experimental.pallas import tpu as pltpu
from jax.sharding import PartitionSpec as P

GX = 128
GY = 128
GZ = 128
MIB = 1024 * 1024


def in_hbm(*arrays):
    return [pltpu.with_memory_space_constraint(a, pltpu.HBM) for a in arrays]


def work(micros):
    return pl.CostEstimate(flops=int(micros * 10**9), bytes_accessed=1024, transcendentals=0)


HIGH = lax.Precision.HIGHEST
ROWS0 = (((0,), (0,)), ((), ()))


def slot_kernel(slabs, planes, block_hbm, cell_hbm, count_hbm, feats_hbm, coords_hbm, map_hbm, bias_hbm, mix_hbm, after_hbm, *refs):
    del after_hbm
    outs = refs[:2]
    (block_ref, cell_ref, count_ref, feats_ref, coords_ref, map_ref, bias_ref, mix_ref, list_ref,
     turned_ref, mixed_ref, part_ref, coef_ref, out_ref, acc_ref, spot_ref, sems) = refs[2:]
    me = lax.axis_index("slab")
    pairs = [(block_hbm, block_ref), (cell_hbm, cell_ref), (count_hbm, count_ref), (feats_hbm, feats_ref),
             (coords_hbm, coords_ref), (map_hbm, map_ref), (bias_hbm, bias_ref), (mix_hbm, mix_ref)]
    copies = [pltpu.make_async_copy(a, b, sems.at[i]) for i, (a, b) in enumerate(pairs)]
    for c in copies: c.start()
    capacity = block_ref.shape[1]
    blocks, channels, points = feats_ref.shape
    hidden = mix_ref.shape[0]
    width = blocks * channels
    base = capacity * channels + 8
    row8 = lax.broadcasted_iota(jnp.int32, (8, points), 0)
    pos_z = (lax.broadcasted_iota(jnp.int32, (GZ, points), 0).astype(jnp.float32) + 0.5) * (1.0 / GZ)
    for c in copies[:7]: c.wait()
    spot_ref[...] = coords_ref[...].astype(jnp.float32)
    for b in range(blocks):
        turned_ref[:, b * channels : (b + 1) * channels] = feats_ref[b].astype(jnp.float32).T.astype(jnp.bfloat16)
    cat = jnp.concatenate([map_ref[...], bias_ref[...], jnp.zeros((4, hidden), jnp.float32)], axis=0)
    live = jnp.int32(0)
    sides = [jnp.where(row8 == 2, 1.0, 0.0)]
    for r in range(slabs):
        peer = lax.rem(me + r, slabs)
        tag_rows = jnp.full((8, points), -1.0, jnp.float32)
        for j in range(capacity):
            n = r * capacity + j
            block = block_ref[peer, j]
            cell = cell_ref[peer, j]
            alive = j < count_ref[peer]
            @pl.when(alive)
            def _():
                list_ref[live] = n
                list_ref[live + 1] = n
            live = live + alive.astype(jnp.int32)
            list_ref[slabs * capacity + 1 + n] = block
            pos_x = ((peer * planes + lax.div(cell, GY)).astype(jnp.float32) + 0.5) * (1.0 / GX)
            pos_y = (lax.rem(cell, GY).astype(jnp.float32) + 0.5) * (1.0 / GY)
            q0 = spot_ref[0, pl.ds(block, 1), :]
            q1 = spot_ref[1, pl.ds(block, 1), :]
            q2 = spot_ref[2, pl.ds(block, 1), :]
            side = jnp.where(row8 == 0, pos_x - q0, jnp.where(row8 == 1, pos_y - q1, jnp.where(row8 == 2, -q2, jnp.where(row8 == 3, 1.0, 0.0))))
            sides.append(side)
            tag_rows = jnp.where(row8 == j, jnp.where(alive, cell, -1).astype(jnp.float32), tag_rows)
        out_ref[r * base + capacity * channels : (r + 1) * base, :] = tag_rows
    parts = lax.dot_general(
        cat, jnp.concatenate(sides, axis=1), ROWS0, precision=HIGH,
        preferred_element_type=jnp.float32,
    )
    coef_ref[...] = parts[:, :points]
    for n in range(slabs * capacity):
        part_ref[n] = parts[:, (n + 1) * points : (n + 2) * points]
    copies[7].wait()
    lane = lax.broadcasted_iota(jnp.int32, (channels, 2 * channels), 1)
    left = turned_ref[...]

    step = max(1, min(hidden // 2, 512 // (blocks * blocks)))

    def mix_step(it, carry):
        for u in range(step):
            h = it * step + u
            mix = mix_ref[h]
            wide = jnp.concatenate([mix, mix], axis=1)
            zero = jnp.zeros_like(wide)
            halves = (jnp.where(lane < channels, wide, zero), jnp.where(lane < channels, zero, wide))
            rows = [jnp.concatenate([halves[b % 2] if b // 2 == t else zero for t in range(blocks // 2)], axis=1) for b in range(blocks)]
            mixed_ref[pl.ds(pl.multiple_of(h * points, points), points), :] = jnp.dot(left, jnp.concatenate(rows, axis=0), preferred_element_type=jnp.float32).astype(jnp.bfloat16)
        return carry
    lax.fori_loop(0, hidden // step, mix_step, 0)

    def pair(it, carry):
        ids = [list_ref[2 * it], list_ref[2 * it + 1]]
        part = 8
        for k in range(0, hidden, part):
            cols = []
            for h in range(k, k + part):
                cell_z = pos_z * coef_ref[h : h + 1, :]
                cols.append(jnp.concatenate([jnp.maximum(cell_z + part_ref[n, h : h + 1, :], 0.0).astype(jnp.bfloat16) for n in ids], axis=0))
            got = jnp.dot(jnp.concatenate(cols, axis=1), mixed_ref[k * points : (k + part) * points, :], preferred_element_type=jnp.float32)
            if k: acc_ref[...] += got
            else: acc_ref[...] = got
        for j, n in enumerate(ids):
            block = list_ref[slabs * capacity + 1 + n]
            pick = acc_ref[j * GZ : (j + 1) * GZ, : 2 * channels]
            for t in range(1, blocks // 2):
                pick = jnp.where(block // 2 == t, acc_ref[j * GZ : (j + 1) * GZ, 2 * t * channels : 2 * (t + 1) * channels], pick)
            turned = pick.T * (1.0 / points)
            start = pl.multiple_of((n // capacity) * base + (n % capacity) * channels, 8)
            out_ref[pl.ds(start, channels), :] = jnp.where(block % 2 == 1, turned[channels:], turned[:channels])
        return carry
    lax.fori_loop(0, (live + 1) // 2, pair, 0)
    for i, out in enumerate(outs):
        out[...] = out_ref[i * out.shape[0] : (i + 1) * out.shape[0], :]

def slot_terms(slot_block, slot_cell, slot_count, feats, coords, offset_map, offset_bias, kernel_mix, planes, after):
    slabs, capacity = slot_block.shape
    blocks, channels, points = feats.shape
    hidden = kernel_mix.shape[0]
    base = capacity * channels + 8
    slots = slabs * capacity
    width = blocks * channels
    slot_limit = hidden * points * width * 2 + (10 if blocks <= 4 else 24) * MIB
    hbm = pl.BlockSpec(memory_space=pltpu.HBM)
    vmem = pl.BlockSpec(memory_space=pltpu.VMEM)
    return pl.pallas_call(
        functools.partial(slot_kernel, slabs, planes),
        out_shape=[jax.ShapeDtypeStruct((slabs * base // 2, GZ), jnp.float32)] * 2,
        in_specs=[hbm] * 8 + [pl.BlockSpec(memory_space=pl.ANY)],
        out_specs=[vmem] * 2,
        scratch_shapes=[
            pltpu.SMEM((slabs, capacity), jnp.int32), pltpu.SMEM((slabs, capacity), jnp.int32), pltpu.SMEM((slabs,), jnp.int32),
            pltpu.VMEM(feats.shape, feats.dtype), pltpu.VMEM(coords.shape, coords.dtype), pltpu.VMEM(offset_map.shape, jnp.float32),
            pltpu.VMEM(offset_bias.shape, jnp.float32), pltpu.VMEM(kernel_mix.shape, kernel_mix.dtype),
            pltpu.SMEM((2 * slots + 2,), jnp.int32),
            pltpu.VMEM((points, width), jnp.bfloat16), pltpu.VMEM((hidden * points, width), jnp.bfloat16),
            pltpu.VMEM((slots, hidden, points), jnp.float32), pltpu.VMEM((hidden, points), jnp.float32),
            pltpu.VMEM((slabs * base, GZ), jnp.float32), pltpu.VMEM((2 * GZ, width), jnp.float32), pltpu.VMEM(coords.shape, jnp.float32),
            pltpu.SemaphoreType.DMA((8,)),
        ],
        compiler_params=pltpu.CompilerParams(vmem_limit_bytes=slot_limit),
        cost_estimate=work(1),
        name="slot_terms",
    )(*in_hbm(slot_block, slot_cell, slot_count, feats, coords, offset_map, offset_bias, kernel_mix),
      after)


def lift_kernel(slabs, capacity, dests, mode_count, *refs):
    terms = refs[:slabs]
    lift_ref, out_ref, token_ref, tag_ref, row_ref, wide_ref, table_ref = refs[slabs:]
    token_ref[...] = jnp.zeros_like(token_ref)
    channels = lift_ref.shape[0]
    kept = channels // dests
    group = slabs * capacity
    slots = slabs * group
    base = capacity * channels + 8
    lanes = table_ref.shape[1]
    tiles = lanes // GZ
    per = out_ref.shape[0] // dests
    cells = lax.broadcasted_iota(jnp.int32, (GZ, lanes), 0)
    lane = lax.broadcasted_iota(jnp.int32, (GZ, lanes), 1)
    step = cells * (lane % mode_count) + jnp.where(lane >= lanes // 2, GZ // 4, 0)
    waves = jnp.cos((step % GZ).astype(jnp.float32) * (2.0 * math.pi / GZ))
    for i in range(kept):
        mine = lane // mode_count % kept == i
        table_ref[i * GZ : (i + 1) * GZ, :] = jnp.where(mine, waves, 0.0)

    def receiver(u, carry):
        starts = [lax.rem(u + s, slabs) * base for s in range(slabs)]

        def tag_of(m):
            first = pl.multiple_of(starts[m // capacity] + capacity * channels, 8)
            return terms[m // capacity][pl.ds(first, 8), :][m % capacity : m % capacity + 1, :]

        def terms_of(m):
            first = pl.multiple_of(starts[m // capacity] + (m % capacity) * channels, 8)
            return terms[m // capacity][pl.ds(first, channels), :]

        tags = [tag_of(m) for m in range(group)]
        for n in range(group):
            live = tags[n] >= 0.0
            summed = jnp.zeros((channels, GZ), jnp.float32)
            leader = live
            for m in range(group):
                same = (tags[m] == tags[n]) & live
                summed = summed + jnp.where(same, terms_of(m), 0.0)
                if m < n:
                    leader = leader & jnp.logical_not(same)
            latent = summed.astype(jnp.bfloat16)
            lifted = jax.nn.gelu(
                lax.dot_general(lift_ref[...], latent, ROWS0, preferred_element_type=jnp.float32)
            )
            row_ref[n] = jnp.where(leader, lifted, 0.0)
            rows = pl.ds(pl.multiple_of((u * group + n) * dests, 8), dests)
            for i in range(kept):
                wide_ref[rows, i * GZ : (i + 1) * GZ] = row_ref[
                    n, pl.ds(i, dests, stride=kept), :
                ]
        tag_ref[pl.ds(pl.multiple_of(u * group, 8), group), :] = jnp.concatenate(tags, axis=0)
        return carry

    lax.fori_loop(0, slabs, receiver, 0, unroll=slabs <= 2)
    modes = jnp.dot(
        wide_ref[...], table_ref[...], precision=HIGH, preferred_element_type=jnp.float32
    )
    for n in range(slots):
        for t in range(tiles):
            out_ref[pl.ds(t * slots + n, dests, stride=per), :] = modes[
                n * dests : (n + 1) * dests, t * GZ : (t + 1) * GZ
            ]
    row = lax.broadcasted_iota(jnp.int32, (slots, GZ), 0)
    lane = lax.broadcasted_iota(jnp.int32, (slots, GZ), 1)
    place = lax.broadcasted_iota(jnp.int32, (8, GZ), 0)
    packed = jnp.zeros((8, GZ), jnp.float32)
    for k in range((slots + GZ - 1) // GZ):
        line = jnp.sum(jnp.where(row == lane + k * GZ, tag_ref[...], 0.0), axis=0, keepdims=True)
        packed = jnp.where(place == k, line, packed)
    for d in range(dests):
        out_ref[d * per + tiles * slots : (d + 1) * per, :] = packed


def lift_slots(terms, lift_weight, capacity, dests, mode_count):
    slabs = len(terms)
    channels = lift_weight.shape[0]
    slots = slabs * slabs * capacity
    kept = channels // dests
    lanes = 2 * kept * mode_count
    per = lanes // GZ * slots + 8
    vmem = pl.BlockSpec(memory_space=pltpu.VMEM)
    return pl.pallas_call(
        functools.partial(lift_kernel, slabs, capacity, dests, mode_count),
        out_shape=[
            jax.ShapeDtypeStruct((dests * per, GZ), jnp.float32),
            jax.ShapeDtypeStruct((8, GZ), jnp.float32),
        ],
        in_specs=[vmem] * (slabs + 1),
        out_specs=[vmem] * 2,
        scratch_shapes=[
            pltpu.VMEM((slots, GZ), jnp.float32),
            pltpu.VMEM((slabs * capacity, channels, GZ), jnp.float32),
            pltpu.VMEM((slots * dests, kept * GZ), jnp.float32),
            pltpu.VMEM((kept * GZ, lanes), jnp.float32),
        ],
        compiler_params=pltpu.CompilerParams(
            vmem_limit_bytes=(8 if slabs <= 2 else 48) * MIB
        ),
        cost_estimate=work(0.1),
        name="lift_slots",
    )(*terms, lift_weight)


def modes_kernel(chips, slabs, slots, planes, scale, group, mode_count, *refs):
    recv_refs = refs[:2]
    out_ref, token_ref, all_ref = refs[2:]
    token_ref[...] = jnp.zeros_like(token_ref)
    samples = 2 * chips
    tiles = all_ref.shape[0]
    total = all_ref.shape[1] // samples
    half = tiles * GZ // 2
    per = recv_refs[0].shape[0] // chips

    device = lax.axis_index("dp")
    slab = lax.axis_index("slab")
    first_x = (slab * 2 + lax.rem(device, 2)) * (total // mode_count)
    spot = lax.broadcasted_iota(jnp.int32, (1, total), 1)
    freq_x = first_x + spot // mode_count
    freq_y = spot % mode_count
    freq_x = jnp.where(freq_x < mode_count // 2, freq_x, freq_x - mode_count)
    freq_y = jnp.where(freq_y < mode_count // 2, freq_y, freq_y - mode_count)
    freq_x, freq_y = freq_x.astype(jnp.float32), freq_y.astype(jnp.float32)

    row = lax.broadcasted_iota(jnp.int32, (slots, GZ), 0)
    lane = lax.broadcasted_iota(jnp.int32, (slots, GZ), 1)
    peer = slab + lax.broadcasted_iota(jnp.int32, (slots, 1), 0) // (slots // slabs)
    plane = jnp.where(peer >= slabs, peer - slabs, peer).astype(jnp.float32) * planes

    def body(p, carry):
        base = pl.multiple_of(ring_chip(lax.div(device, 2), p, chips) * per, 8)
        for core, ref in enumerate(recv_refs):
            plain = jnp.concatenate(
                [ref[pl.ds(base + u * slots, slots), :] for u in range(tiles)], axis=1
            )
            packed = ref[pl.ds(base + tiles * slots, 8), :]
            tag = jnp.zeros((slots, 1), jnp.float32)
            for k in range((slots + GZ - 1) // GZ):
                tag = tag + jnp.sum(
                    jnp.where(row == lane + k * GZ, packed[k : k + 1, :], 0.0),
                    axis=1,
                    keepdims=True,
                )
            tag = jnp.maximum(tag, 0.0)
            local_x = jnp.floor(tag * (1.0 / GY))
            turns = (local_x + plane) * (1.0 / GX) * freq_x + (
                tag - local_x * GY
            ) * (1.0 / GY) * freq_y
            angle = (turns - jnp.floor(turns)) * (2.0 * math.pi)
            crossed = jnp.concatenate([plain[:, half:], -plain[:, :half]], axis=1)
            modes = lax.dot_general(
                jnp.concatenate([jnp.cos(angle), jnp.sin(angle)], axis=0),
                jnp.concatenate([plain, crossed], axis=0),
                ROWS0,
                precision=HIGH,
                preferred_element_type=jnp.float32,
            )
            for u in range(tiles):
                all_ref[u, pl.ds(2 * p + core, total, stride=samples), :] = (
                    modes[:, u * GZ : (u + 1) * GZ] * scale
                )
        return carry

    lax.fori_loop(0, chips, body, 0, unroll=4)

    span = group * samples
    for block in range(total // group):
        for u in range(tiles):
            out_ref[block, u * GZ : (u + 1) * GZ, :] = all_ref[
                u, block * span : (block + 1) * span, :
            ].T.astype(jnp.bfloat16)


def sample_modes(recv, chips, slabs, slots, planes, scale, group, total, mode_count, lanes):
    samples = 2 * chips
    vmem = pl.BlockSpec(memory_space=pltpu.VMEM)
    return pl.pallas_call(
        functools.partial(modes_kernel, chips, slabs, slots, planes, scale, group, mode_count),
        out_shape=[
            jax.ShapeDtypeStruct((total // group, lanes, group * samples), jnp.bfloat16),
            jax.ShapeDtypeStruct((8, GZ), jnp.float32),
        ],
        in_specs=[vmem] * len(recv),
        out_specs=[vmem] * 2,
        scratch_shapes=[pltpu.VMEM((lanes // GZ, total * samples, GZ), jnp.float32)],
        compiler_params=pltpu.CompilerParams(vmem_limit_bytes=(8 if slabs <= 2 else 32) * MIB),
        cost_estimate=work(0.2),
        name="sample_modes",
    )(*recv)


def spread_kernel(depth, modes_ref, after_ref, out_ref, pick_ref, mask_ref):
    del after_ref
    group = out_ref.shape[0]
    span = out_ref.shape[2]

    @pl.when(pl.program_id(0) == 0)
    def _():
        row = lax.broadcasted_iota(jnp.int32, pick_ref.shape, 0)
        col = lax.broadcasted_iota(jnp.int32, pick_ref.shape, 1)
        pick_ref[...] = jnp.where(row == col // depth, 1.0, 0.0).astype(jnp.bfloat16)
        row = lax.broadcasted_iota(jnp.int32, mask_ref.shape, 0)
        col = lax.broadcasted_iota(jnp.int32, mask_ref.shape, 1)
        mask_ref[...] = jnp.where(row % depth == col % depth, 1.0, 0.0)

    for g in range(group):
        left = jnp.dot(
            modes_ref[0], pick_ref[:, g * span : (g + 1) * span],
            preferred_element_type=jnp.float32,
        )
        out_ref[g] = (left * mask_ref[...]).astype(jnp.bfloat16)


def spread_modes(modes, group, depth, after):
    blocks, lanes, columns = modes.shape
    span = columns // group * depth
    return pl.pallas_call(
        functools.partial(spread_kernel, depth),
        out_shape=jax.ShapeDtypeStruct((blocks * group, lanes, span), jnp.bfloat16),
        grid=(blocks,),
        in_specs=[
            pl.BlockSpec((1, lanes, columns), lambda s: (s, 0, 0)),
            pl.BlockSpec(memory_space=pl.ANY),
        ],
        out_specs=pl.BlockSpec((group, lanes, span), lambda s: (s, 0, 0)),
        scratch_shapes=[
            pltpu.VMEM((columns, group * span), jnp.bfloat16),
            pltpu.VMEM((lanes, span), jnp.float32),
        ],
        compiler_params=pltpu.CompilerParams(vmem_limit_bytes=8 * MIB),
        cost_estimate=work(0.2),
        name="spread_modes",
    )(modes, after)


def grad_kernel(chunk, chunks, depth, firsts, aliased, modes_ref, *refs):
    count = 1 + max(index for index, _ in firsts)
    out_hbm, other_ref, own_ref, sems = refs[count + aliased :]
    half_rows = modes_ref.shape[1] // 2
    kept, size, width = other_ref.shape
    half = width // 2
    core = lax.rem(lax.axis_index("dp"), 2)
    first = core == 0
    group = min(16, size // depth)
    tile = group * depth
    steps = size // tile

    def write(s):
        start = pl.multiple_of(s * tile, tile)
        place = pl.multiple_of((core * chunks + chunk) * size + s * tile, tile)
        return pltpu.make_async_copy(
            own_ref.at[:, pl.ds(start, tile), :], out_hbm.at[:, pl.ds(place, tile), :], sems.at[s]
        )

    for s in range(steps):
        for g in range(group):
            start = s * tile + g * depth
            right = jnp.concatenate(
                [refs[i][at + start : at + start + depth, :] for i, at in firsts], axis=0
            )
            left = modes_ref[(chunk * steps + s) * group + g]
            both = jnp.dot(left, right, preferred_element_type=jnp.float32)
            plain, turned = both[:half_rows], both[half_rows:]
            total = plain + jnp.concatenate([turned[:, half:], -turned[:, :half]], axis=1)
            low, high = total[: half_rows // 2], total[half_rows // 2 :]
            own, other = jnp.where(first, low, high), jnp.where(first, high, low)
            for i in range(kept):
                own_ref[i, pl.ds(start, depth), :] = own[i * depth : (i + 1) * depth]
                other_ref[i, pl.ds(start, depth), :] = other[i * depth : (i + 1) * depth]
        write(s).start()
    for s in range(steps):
        write(s).wait()


def grad_chunk(modes, rows, kept, depth, chunk, chunks, previous):
    arrays, firsts = [], []
    for array, first in rows:
        if not any(array is known for known in arrays):
            arrays.append(array)
        firsts.append(([array is known for known in arrays].index(True), first))
    size, width = arrays[0].shape[0] // chunks, arrays[0].shape[1]
    hbm = pl.BlockSpec(memory_space=pl.ANY)
    vmem = pl.BlockSpec(memory_space=pltpu.VMEM)
    operands = [modes, *arrays]
    in_specs = [vmem] * len(operands)
    aliases = {}
    if previous is not None:
        in_specs.append(hbm)
        aliases = {len(operands): 0}
        operands.append(previous)
    steps = size // depth // min(16, size // depth)
    return pl.pallas_call(
        functools.partial(grad_kernel, chunk, chunks, depth, firsts, int(previous is not None)),
        out_shape=[
            jax.ShapeDtypeStruct((kept, 2 * chunks * size, width), jnp.float32),
            jax.ShapeDtypeStruct((kept, size, width), jnp.float32),
        ],
        in_specs=in_specs,
        out_specs=[hbm, vmem],
        scratch_shapes=[
            pltpu.VMEM((kept, size, width), jnp.float32),
            pltpu.SemaphoreType.DMA((steps,)),
        ],
        input_output_aliases=aliases,
        compiler_params=pltpu.CompilerParams(vmem_limit_bytes=12 * MIB),
        cost_estimate=work(1),
        name="grad_chunk",
    )(*operands)


def place_kernel(chunk, chunks, part_ref, old_hbm, out_hbm, sems):
    del old_hbm
    kept, size, _ = part_ref.shape
    core = lax.rem(lax.axis_index("dp"), 2)
    start = pl.multiple_of(((1 - core) * chunks + chunk) * size, size)
    cuts = sems.shape[0] // kept
    rows = size // cuts
    copies = [
        pltpu.make_async_copy(
            part_ref.at[i, pl.ds(c * rows, rows), :],
            out_hbm.at[i, pl.ds(start + c * rows, rows), :],
            sems.at[i * cuts + c],
        )
        for i in range(kept)
        for c in range(cuts)
    ]
    for copy in copies:
        copy.start()
    for copy in copies:
        copy.wait()


def place_chunk(part, result, chunk, chunks):
    hbm = pl.BlockSpec(memory_space=pl.ANY)
    return pl.pallas_call(
        functools.partial(place_kernel, chunk, chunks),
        out_shape=jax.ShapeDtypeStruct(result.shape, result.dtype),
        in_specs=[pl.BlockSpec(memory_space=pltpu.VMEM), hbm],
        out_specs=hbm,
        scratch_shapes=[pltpu.SemaphoreType.DMA((part.shape[0],))],
        input_output_aliases={1: 0},
        compiler_params=pltpu.CompilerParams(vmem_limit_bytes=8 * MIB),
        cost_estimate=work(0.2),
        name="place_chunk",
    )(part, result)


def cast_kernel(parts, rows_hbm, keep_ref, give_ref, held_ref, sems):
    size = held_ref.shape[0] // (2 * parts)
    core = lax.rem(lax.axis_index("dp"), 2)
    halves = [(keep_ref, core * parts), (give_ref, (1 - core) * parts)]
    copies, jobs = [], []
    for h, (out, first) in enumerate(halves):
        for i in range(parts):
            source = pl.ds(pl.multiple_of((first + i) * size, size), size)
            spot = pl.ds((h * parts + i) * size, size)
            copies.append(
                pltpu.make_async_copy(
                    rows_hbm.at[source, :], held_ref.at[spot, :], sems.at[h * parts + i]
                )
            )
            jobs.append((out, pl.ds(i * size, size), spot))
    for copy in copies:
        copy.start()
    for copy, (out, place, spot) in zip(copies, jobs):
        copy.wait()
        out[place, :] = held_ref[spot, :].astype(jnp.bfloat16)


def cast_rows(rows):
    parts = 2
    total, width = rows.shape
    return pl.pallas_call(
        functools.partial(cast_kernel, parts),
        out_shape=[jax.ShapeDtypeStruct((total // 2, width), jnp.bfloat16)] * 2,
        in_specs=[pl.BlockSpec(memory_space=pltpu.HBM)],
        out_specs=[pl.BlockSpec(memory_space=pltpu.VMEM)] * 2,
        scratch_shapes=[
            pltpu.VMEM(rows.shape, jnp.float32),
            pltpu.SemaphoreType.DMA((2 * parts,)),
        ],
        compiler_params=pltpu.CompilerParams(vmem_limit_bytes=8 * MIB),
        cost_estimate=work(0.1),
        name="cast_rows",
    )(*in_hbm(rows))


def chip_ring(chips):
    order = list(range(0, chips, 2))
    return order + [c for c in range(chips - 1, 0, -1) if c % 2]


def ring_perm(chips, step):
    order = chip_ring(chips)
    return [
        (2 * order[p] + core, 2 * order[(p + step) % chips] + core)
        for p in range(chips)
        for core in (0, 1)
    ]


def ring_chip(chip, p, chips):
    up = (chips + 1) // 2
    place = jnp.where(lax.rem(chip, 2) == 0, lax.div(chip, 2), chips - 1 - lax.div(chip, 2))
    spot = lax.rem(place - p + chips, chips)
    return jnp.where(spot < up, 2 * spot, 2 * (chips - 1 - spot) + 1)


def joint_kernel(spans, total, *refs):
    for parts, new in zip(spans, refs[total:]):
        place = 0
        for source, start, size in parts:
            new[place : place + size] = refs[source][start : start + size]
            place += size


def joint(pieces, *after):
    arrays, spans = [], []

    def known(array):
        for i, other in enumerate(arrays):
            if other is array:
                return i
        arrays.append(array)
        return len(arrays) - 1

    for piece in pieces:
        parts = piece if isinstance(piece, list) else [piece]
        parts = [p if isinstance(p, tuple) else (p, 0, p.shape[0]) for p in parts]
        spans.append([(known(array), start, size) for array, start, size in parts])
    vmem = pl.BlockSpec(memory_space=pltpu.VMEM)
    operands = [*arrays, *after]
    return pl.pallas_call(
        functools.partial(joint_kernel, spans, len(operands)),
        out_shape=[
            jax.ShapeDtypeStruct(
                (sum(part[2] for part in parts), *arrays[parts[0][0]].shape[1:]),
                arrays[parts[0][0]].dtype,
            )
            for parts in spans
        ],
        in_specs=[vmem] * len(operands),
        out_specs=[vmem] * len(spans),
        compiler_params=pltpu.CompilerParams(vmem_limit_bytes=4 * MIB),
        cost_estimate=work(0.01),
        name="joint",
    )(*operands)


def per_device(
    point_feats, point_coords, slot_block, slot_cell, slot_count, cotangent, offset_map,
    offset_bias, kernel_mix, lift_weight,
):
    slabs = lax.axis_size("slab")
    devices = lax.axis_size("dp")
    channels = point_feats.shape[2]
    mode_count = cotangent.shape[2]
    capacity = slot_block.shape[3]
    width = cotangent.shape[4]
    planes = GX // slabs
    kept = channels // devices
    slots = slabs * slabs * capacity
    local_x = cotangent.shape[1]
    total = local_x // 2 * mode_count
    chunks = 2
    group = min(8, total // chunks)
    chips = devices // 2
    far = chips // 2

    scale = 1.0 / math.sqrt(GZ * slabs * slabs * capacity)

    def up(rows):
        return lax.ppermute(rows, "dp", ring_perm(chips, 1))

    def down(rows):
        return lax.ppermute(rows, "dp", ring_perm(chips, -1))

    def swap(rows):
        return lax.ppermute(rows, "dp", [(d, d ^ 1) for d in range(devices)])

    own, given = cast_rows(cotangent[0].reshape(-1, width))
    size = own.shape[0]
    ups, downs = [up(own)], [down(own)]
    twin = swap(given)
    ups.append(up(twin))
    downs.append(down(twin))

    sent = slot_terms(
        slot_block[0, 0], slot_cell[0, 0], slot_count[0, 0], point_feats[0],
        jnp.swapaxes(point_coords[0], 0, 1), offset_map.T, offset_bias[None], kernel_mix, planes,
        twin,
    )
    pair = {}
    *outs, first, second = joint([*ups, *downs, *sent])
    pair[1], pair[chips - 1], sent = outs[:2], outs[2:], [first, second]

    pair[2] = [up(rows) for rows in pair[1]]
    pair[chips - 2] = [down(rows) for rows in pair[chips - 1]]
    terms = [sent] + [
        [lax.ppermute(x, "slab", [(t, (t + s) % slabs) for t in range(slabs)]) for x in sent]
        for s in range(1, slabs)
    ]
    terms = joint(terms)
    payload, lift_done = lift_slots(terms, lift_weight, capacity, chips, mode_count)
    recv = lax.all_to_all(
        payload.reshape(chips, -1, GZ), "dp", split_axis=0, concat_axis=0, tiled=True,
        axis_index_groups=[list(range(c, devices, 2)) for c in range(2)],
    ).reshape(payload.shape)
    outs = joint([*pair[2], *pair[chips - 2]], lift_done)
    sent_on = {2: outs[:2], chips - 2: outs[2:]}

    for s in range(3, far):
        pair[s] = [up(rows) for rows in sent_on.get(s - 1, pair[s - 1])]
        pair[chips - s] = [
            down(rows) for rows in sent_on.get(chips - s + 1, pair[chips - s + 1])
        ]
    modes, modes_done = sample_modes(
        [recv, swap(recv)], chips, slabs, slots, planes, scale, group, total, mode_count,
        4 * kept * mode_count,
    )
    half = size // 2
    first, second = joint(
        [
            [(rows, 0, half) for rows in pair[far - 1]],
            [(rows, half, half) for rows in pair[far + 1]],
        ],
        modes_done,
    )

    ends = [up(first), down(second)]
    modes = spread_modes(modes, group, mode_count, first)

    result, parts = None, []
    for c in range(chunks):
        rows = [(own, c * half), (twin, c * half)]
        for p in range(1, chips):
            if p == far:
                rows += [(ends[c], 0), (ends[c], half)]
            else:
                rows += [(array, c * half) for array in pair[p]]
        result, part = grad_chunk(modes, rows, kept, mode_count, c, chunks, result)
        parts.append(swap(part))
    for c, part in enumerate(parts):
        result = place_chunk(part, result, c, chunks)
    return result.reshape(kept, local_x, mode_count, mode_count, width)


def solution(mesh):
    placed = (
        P("dp", "slab", None, None),
        P("dp", "slab", None, None),
        P("dp", "slab", None, None),
        P("dp", "slab", None, None),
        P("dp", "slab", None),
        P("dp", "slab", None, None, None),
        P(),
        P(),
        P(),
        P(),
    )
    return jax.shard_map(
        per_device,
        mesh=mesh,
        in_specs=placed,
        out_specs=P("dp", "slab", None, None, None),
        check_vma=False,
    )
```

```python
import functools
import math

import jax
import jax.numpy as jnp
from jax import lax
from jax.experimental import pallas as pl
from jax.experimental.pallas import tpu as pltpu
from jax.sharding import PartitionSpec as P

GX = 128
GY = 128
GZ = 128
MIB = 1024 * 1024


def in_hbm(*arrays):
    return [pltpu.with_memory_space_constraint(a, pltpu.HBM) for a in arrays]


def work(micros):
    return pl.CostEstimate(flops=int(micros * 10**9), bytes_accessed=1024, transcendentals=0)


HIGH = lax.Precision.HIGHEST
ROWS0 = (((0,), (0,)), ((), ()))


def slot_kernel(slabs, planes, block_hbm, cell_hbm, count_hbm, feats_hbm, coords_hbm, map_hbm, bias_hbm, mix_hbm, after_hbm, *refs):
    del after_hbm
    outs = refs[:2]
    (block_ref, cell_ref, count_ref, feats_ref, coords_ref, map_ref, bias_ref, mix_ref, list_ref,
     turned_ref, mixed_ref, part_ref, coef_ref, out_ref, acc_ref, spot_ref, sems) = refs[2:]
    me = lax.axis_index("slab")
    pairs = [(block_hbm, block_ref), (cell_hbm, cell_ref), (count_hbm, count_ref), (feats_hbm, feats_ref),
             (coords_hbm, coords_ref), (map_hbm, map_ref), (bias_hbm, bias_ref), (mix_hbm, mix_ref)]
    copies = [pltpu.make_async_copy(a, b, sems.at[i]) for i, (a, b) in enumerate(pairs)]
    for c in copies: c.start()
    capacity = block_ref.shape[1]
    blocks, channels, points = feats_ref.shape
    hidden = mix_ref.shape[0]
    width = blocks * channels
    base = capacity * channels + 8
    row8 = lax.broadcasted_iota(jnp.int32, (8, points), 0)
    pos_z = (lax.broadcasted_iota(jnp.int32, (GZ, points), 0).astype(jnp.float32) + 0.5) * (1.0 / GZ)
    for c in copies[:7]: c.wait()
    spot_ref[...] = coords_ref[...].astype(jnp.float32)
    for b in range(blocks):
        turned_ref[:, b * channels : (b + 1) * channels] = feats_ref[b].astype(jnp.float32).T.astype(jnp.bfloat16)
    cat = jnp.concatenate([map_ref[...], bias_ref[...], jnp.zeros((4, hidden), jnp.float32)], axis=0)
    live = jnp.int32(0)
    sides = [jnp.where(row8 == 2, 1.0, 0.0)]
    for r in range(slabs):
        peer = lax.rem(me + r, slabs)
        tag_rows = jnp.full((8, points), -1.0, jnp.float32)
        for j in range(capacity):
            n = r * capacity + j
            block = block_ref[peer, j]
            cell = cell_ref[peer, j]
            alive = j < count_ref[peer]
            @pl.when(alive)
            def _():
                list_ref[live] = n
                list_ref[live + 1] = n
            live = live + alive.astype(jnp.int32)
            list_ref[slabs * capacity + 1 + n] = block
            pos_x = ((peer * planes + lax.div(cell, GY)).astype(jnp.float32) + 0.5) * (1.0 / GX)
            pos_y = (lax.rem(cell, GY).astype(jnp.float32) + 0.5) * (1.0 / GY)
            q0 = spot_ref[0, pl.ds(block, 1), :]
            q1 = spot_ref[1, pl.ds(block, 1), :]
            q2 = spot_ref[2, pl.ds(block, 1), :]
            side = jnp.where(row8 == 0, pos_x - q0, jnp.where(row8 == 1, pos_y - q1, jnp.where(row8 == 2, -q2, jnp.where(row8 == 3, 1.0, 0.0))))
            sides.append(side)
            tag_rows = jnp.where(row8 == j, jnp.where(alive, cell, -1).astype(jnp.float32), tag_rows)
        out_ref[r * base + capacity * channels : (r + 1) * base, :] = tag_rows
    parts = lax.dot_general(
        cat, jnp.concatenate(sides, axis=1), ROWS0, precision=HIGH,
        preferred_element_type=jnp.float32,
    )
    coef_ref[...] = parts[:, :points]
    for n in range(slabs * capacity):
        part_ref[n] = parts[:, (n + 1) * points : (n + 2) * points]
    copies[7].wait()
    lane = lax.broadcasted_iota(jnp.int32, (channels, 2 * channels), 1)
    left = turned_ref[...]

    step = max(1, min(hidden // 2, 512 // (blocks * blocks)))

    def mix_step(it, carry):
        for u in range(step):
            h = it * step + u
            mix = mix_ref[h]
            wide = jnp.concatenate([mix, mix], axis=1)
            zero = jnp.zeros_like(wide)
            halves = (jnp.where(lane < channels, wide, zero), jnp.where(lane < channels, zero, wide))
            rows = [jnp.concatenate([halves[b % 2] if b // 2 == t else zero for t in range(blocks // 2)], axis=1) for b in range(blocks)]
            mixed_ref[pl.ds(pl.multiple_of(h * points, points), points), :] = jnp.dot(left, jnp.concatenate(rows, axis=0), preferred_element_type=jnp.float32).astype(jnp.bfloat16)
        return carry
    lax.fori_loop(0, hidden // step, mix_step, 0)

    def pair(it, carry):
        ids = [list_ref[2 * it], list_ref[2 * it + 1]]
        part = 8
        for k in range(0, hidden, part):
            cols = []
            for h in range(k, k + part):
                cell_z = pos_z * coef_ref[h : h + 1, :]
                cols.append(jnp.concatenate([jnp.maximum(cell_z + part_ref[n, h : h + 1, :], 0.0).astype(jnp.bfloat16) for n in ids], axis=0))
            got = jnp.dot(jnp.concatenate(cols, axis=1), mixed_ref[k * points : (k + part) * points, :], preferred_element_type=jnp.float32)
            if k: acc_ref[...] += got
            else: acc_ref[...] = got
        for j, n in enumerate(ids):
            block = list_ref[slabs * capacity + 1 + n]
            pick = acc_ref[j * GZ : (j + 1) * GZ, : 2 * channels]
            for t in range(1, blocks // 2):
                pick = jnp.where(block // 2 == t, acc_ref[j * GZ : (j + 1) * GZ, 2 * t * channels : 2 * (t + 1) * channels], pick)
            turned = pick.T * (1.0 / points)
            start = pl.multiple_of((n // capacity) * base + (n % capacity) * channels, 8)
            out_ref[pl.ds(start, channels), :] = jnp.where(block % 2 == 1, turned[channels:], turned[:channels])
        return carry
    lax.fori_loop(0, (live + 1) // 2, pair, 0)
    for i, out in enumerate(outs):
        out[...] = out_ref[i * out.shape[0] : (i + 1) * out.shape[0], :]

def slot_terms(slot_block, slot_cell, slot_count, feats, coords, offset_map, offset_bias, kernel_mix, planes, after):
    slabs, capacity = slot_block.shape
    blocks, channels, points = feats.shape
    hidden = kernel_mix.shape[0]
    base = capacity * channels + 8
    slots = slabs * capacity
    width = blocks * channels
    slot_limit = hidden * points * width * 2 + (10 if blocks <= 4 else 24) * MIB
    hbm = pl.BlockSpec(memory_space=pltpu.HBM)
    vmem = pl.BlockSpec(memory_space=pltpu.VMEM)
    return pl.pallas_call(
        functools.partial(slot_kernel, slabs, planes),
        out_shape=[jax.ShapeDtypeStruct((slabs * base // 2, GZ), jnp.float32)] * 2,
        in_specs=[hbm] * 8 + [pl.BlockSpec(memory_space=pl.ANY)],
        out_specs=[vmem] * 2,
        scratch_shapes=[
            pltpu.SMEM((slabs, capacity), jnp.int32), pltpu.SMEM((slabs, capacity), jnp.int32), pltpu.SMEM((slabs,), jnp.int32),
            pltpu.VMEM(feats.shape, feats.dtype), pltpu.VMEM(coords.shape, coords.dtype), pltpu.VMEM(offset_map.shape, jnp.float32),
            pltpu.VMEM(offset_bias.shape, jnp.float32), pltpu.VMEM(kernel_mix.shape, kernel_mix.dtype),
            pltpu.SMEM((2 * slots + 2,), jnp.int32),
            pltpu.VMEM((points, width), jnp.bfloat16), pltpu.VMEM((hidden * points, width), jnp.bfloat16),
            pltpu.VMEM((slots, hidden, points), jnp.float32), pltpu.VMEM((hidden, points), jnp.float32),
            pltpu.VMEM((slabs * base, GZ), jnp.float32), pltpu.VMEM((2 * GZ, width), jnp.float32), pltpu.VMEM(coords.shape, jnp.float32),
            pltpu.SemaphoreType.DMA((8,)),
        ],
        compiler_params=pltpu.CompilerParams(vmem_limit_bytes=slot_limit),
        cost_estimate=work(1),
        name="slot_terms",
    )(*in_hbm(slot_block, slot_cell, slot_count, feats, coords, offset_map, offset_bias, kernel_mix),
      after)


def lift_kernel(slabs, capacity, dests, mode_count, *refs):
    terms = refs[:slabs]
    lift_ref, out_ref, token_ref, tag_ref, row_ref, wide_ref, table_ref = refs[slabs:]
    token_ref[...] = jnp.zeros_like(token_ref)
    channels = lift_ref.shape[0]
    kept = channels // dests
    group = slabs * capacity
    slots = slabs * group
    base = capacity * channels + 8
    lanes = table_ref.shape[1]
    tiles = lanes // GZ
    per = out_ref.shape[0] // dests
    cells = lax.broadcasted_iota(jnp.int32, (GZ, lanes), 0)
    lane = lax.broadcasted_iota(jnp.int32, (GZ, lanes), 1)
    step = cells * (lane % mode_count) + jnp.where(lane >= lanes // 2, GZ // 4, 0)
    waves = jnp.cos((step % GZ).astype(jnp.float32) * (2.0 * math.pi / GZ))
    for i in range(kept):
        mine = lane // mode_count % kept == i
        table_ref[i * GZ : (i + 1) * GZ, :] = jnp.where(mine, waves, 0.0)

    def receiver(u, carry):
        starts = [lax.rem(u + s, slabs) * base for s in range(slabs)]

        def tag_of(m):
            first = pl.multiple_of(starts[m // capacity] + capacity * channels, 8)
            return terms[m // capacity][pl.ds(first, 8), :][m % capacity : m % capacity + 1, :]

        def terms_of(m):
            first = pl.multiple_of(starts[m // capacity] + (m % capacity) * channels, 8)
            return terms[m // capacity][pl.ds(first, channels), :]

        tags = [tag_of(m) for m in range(group)]
        for n in range(group):
            live = tags[n] >= 0.0
            summed = jnp.zeros((channels, GZ), jnp.float32)
            leader = live
            for m in range(group):
                same = (tags[m] == tags[n]) & live
                summed = summed + jnp.where(same, terms_of(m), 0.0)
                if m < n:
                    leader = leader & jnp.logical_not(same)
            latent = summed.astype(jnp.bfloat16)
            lifted = jax.nn.gelu(
                lax.dot_general(lift_ref[...], latent, ROWS0, preferred_element_type=jnp.float32)
            )
            row_ref[n] = jnp.where(leader, lifted, 0.0)
            rows = pl.ds(pl.multiple_of((u * group + n) * dests, 8), dests)
            for i in range(kept):
                wide_ref[rows, i * GZ : (i + 1) * GZ] = row_ref[
                    n, pl.ds(i, dests, stride=kept), :
                ]
        tag_ref[pl.ds(pl.multiple_of(u * group, 8), group), :] = jnp.concatenate(tags, axis=0)
        return carry

    lax.fori_loop(0, slabs, receiver, 0, unroll=slabs <= 2)
    modes = jnp.dot(
        wide_ref[...], table_ref[...], precision=HIGH, preferred_element_type=jnp.float32
    )
    for n in range(slots):
        for t in range(tiles):
            out_ref[pl.ds(t * slots + n, dests, stride=per), :] = modes[
                n * dests : (n + 1) * dests, t * GZ : (t + 1) * GZ
            ]
    row = lax.broadcasted_iota(jnp.int32, (slots, GZ), 0)
    lane = lax.broadcasted_iota(jnp.int32, (slots, GZ), 1)
    place = lax.broadcasted_iota(jnp.int32, (8, GZ), 0)
    packed = jnp.zeros((8, GZ), jnp.float32)
    for k in range((slots + GZ - 1) // GZ):
        line = jnp.sum(jnp.where(row == lane + k * GZ, tag_ref[...], 0.0), axis=0, keepdims=True)
        packed = jnp.where(place == k, line, packed)
    for d in range(dests):
        out_ref[d * per + tiles * slots : (d + 1) * per, :] = packed


def lift_slots(terms, lift_weight, capacity, dests, mode_count):
    slabs = len(terms)
    channels = lift_weight.shape[0]
    slots = slabs * slabs * capacity
    kept = channels // dests
    lanes = 2 * kept * mode_count
    per = lanes // GZ * slots + 8
    vmem = pl.BlockSpec(memory_space=pltpu.VMEM)
    return pl.pallas_call(
        functools.partial(lift_kernel, slabs, capacity, dests, mode_count),
        out_shape=[
            jax.ShapeDtypeStruct((dests * per, GZ), jnp.float32),
            jax.ShapeDtypeStruct((8, GZ), jnp.float32),
        ],
        in_specs=[vmem] * (slabs + 1),
        out_specs=[vmem] * 2,
        scratch_shapes=[
            pltpu.VMEM((slots, GZ), jnp.float32),
            pltpu.VMEM((slabs * capacity, channels, GZ), jnp.float32),
            pltpu.VMEM((slots * dests, kept * GZ), jnp.float32),
            pltpu.VMEM((kept * GZ, lanes), jnp.float32),
        ],
        compiler_params=pltpu.CompilerParams(
            vmem_limit_bytes=(6 if slabs <= 2 else 48) * MIB
        ),
        cost_estimate=work(0.1),
        name="lift_slots",
    )(*terms, lift_weight)


def modes_kernel(chips, slabs, slots, planes, scale, group, mode_count, *refs):
    recv_refs = refs[:2]
    out_ref, token_ref, all_ref = refs[2:]
    token_ref[...] = jnp.zeros_like(token_ref)
    samples = 2 * chips
    tiles = all_ref.shape[0]
    total = all_ref.shape[1] // samples
    half = tiles * GZ // 2
    per = recv_refs[0].shape[0] // chips

    device = lax.axis_index("dp")
    slab = lax.axis_index("slab")
    first_x = (slab * 2 + lax.rem(device, 2)) * (total // mode_count)
    spot = lax.broadcasted_iota(jnp.int32, (1, total), 1)
    freq_x = first_x + spot // mode_count
    freq_y = spot % mode_count
    freq_x = jnp.where(freq_x < mode_count // 2, freq_x, freq_x - mode_count)
    freq_y = jnp.where(freq_y < mode_count // 2, freq_y, freq_y - mode_count)
    freq_x, freq_y = freq_x.astype(jnp.float32), freq_y.astype(jnp.float32)

    row = lax.broadcasted_iota(jnp.int32, (slots, GZ), 0)
    lane = lax.broadcasted_iota(jnp.int32, (slots, GZ), 1)
    peer = slab + lax.broadcasted_iota(jnp.int32, (slots, 1), 0) // (slots // slabs)
    plane = jnp.where(peer >= slabs, peer - slabs, peer).astype(jnp.float32) * planes

    def body(p, carry):
        base = pl.multiple_of(ring_chip(lax.div(device, 2), p, chips) * per, 8)
        for core, ref in enumerate(recv_refs):
            plain = jnp.concatenate(
                [ref[pl.ds(base + u * slots, slots), :] for u in range(tiles)], axis=1
            )
            packed = ref[pl.ds(base + tiles * slots, 8), :]
            tag = jnp.zeros((slots, 1), jnp.float32)
            for k in range((slots + GZ - 1) // GZ):
                tag = tag + jnp.sum(
                    jnp.where(row == lane + k * GZ, packed[k : k + 1, :], 0.0),
                    axis=1,
                    keepdims=True,
                )
            tag = jnp.maximum(tag, 0.0)
            local_x = jnp.floor(tag * (1.0 / GY))
            turns = (local_x + plane) * (1.0 / GX) * freq_x + (
                tag - local_x * GY
            ) * (1.0 / GY) * freq_y
            angle = (turns - jnp.floor(turns)) * (2.0 * math.pi)
            crossed = jnp.concatenate([plain[:, half:], -plain[:, :half]], axis=1)
            modes = lax.dot_general(
                jnp.concatenate([jnp.cos(angle), jnp.sin(angle)], axis=0),
                jnp.concatenate([plain, crossed], axis=0),
                ROWS0,
                precision=HIGH,
                preferred_element_type=jnp.float32,
            )
            for u in range(tiles):
                all_ref[u, pl.ds(2 * p + core, total, stride=samples), :] = (
                    modes[:, u * GZ : (u + 1) * GZ] * scale
                )
        return carry

    lax.fori_loop(0, chips, body, 0, unroll=4)

    span = group * samples
    for block in range(total // group):
        for u in range(tiles):
            out_ref[block, u * GZ : (u + 1) * GZ, :] = all_ref[
                u, block * span : (block + 1) * span, :
            ].T.astype(jnp.bfloat16)


def sample_modes(recv, chips, slabs, slots, planes, scale, group, total, mode_count, lanes):
    samples = 2 * chips
    vmem = pl.BlockSpec(memory_space=pltpu.VMEM)
    return pl.pallas_call(
        functools.partial(modes_kernel, chips, slabs, slots, planes, scale, group, mode_count),
        out_shape=[
            jax.ShapeDtypeStruct((total // group, lanes, group * samples), jnp.bfloat16),
            jax.ShapeDtypeStruct((8, GZ), jnp.float32),
        ],
        in_specs=[vmem] * len(recv),
        out_specs=[vmem] * 2,
        scratch_shapes=[pltpu.VMEM((lanes // GZ, total * samples, GZ), jnp.float32)],
        compiler_params=pltpu.CompilerParams(vmem_limit_bytes=(5 if slabs <= 2 else 32) * MIB),
        cost_estimate=work(0.2),
        name="sample_modes",
    )(*recv)


def spread_kernel(depth, modes_ref, after_ref, out_ref, pick_ref, mask_ref):
    del after_ref
    group = out_ref.shape[0]
    span = out_ref.shape[2]

    @pl.when(pl.program_id(0) == 0)
    def _():
        row = lax.broadcasted_iota(jnp.int32, pick_ref.shape, 0)
        col = lax.broadcasted_iota(jnp.int32, pick_ref.shape, 1)
        pick_ref[...] = jnp.where(row == col // depth, 1.0, 0.0).astype(jnp.bfloat16)
        row = lax.broadcasted_iota(jnp.int32, mask_ref.shape, 0)
        col = lax.broadcasted_iota(jnp.int32, mask_ref.shape, 1)
        mask_ref[...] = jnp.where(row % depth == col % depth, 1.0, 0.0)

    for g in range(group):
        left = jnp.dot(
            modes_ref[0], pick_ref[:, g * span : (g + 1) * span],
            preferred_element_type=jnp.float32,
        )
        out_ref[g] = (left * mask_ref[...]).astype(jnp.bfloat16)


def spread_modes(modes, group, depth, after):
    blocks, lanes, columns = modes.shape
    span = columns // group * depth
    return pl.pallas_call(
        functools.partial(spread_kernel, depth),
        out_shape=jax.ShapeDtypeStruct((blocks * group, lanes, span), jnp.bfloat16),
        grid=(blocks,),
        in_specs=[
            pl.BlockSpec((1, lanes, columns), lambda s: (s, 0, 0)),
            pl.BlockSpec(memory_space=pl.ANY),
        ],
        out_specs=pl.BlockSpec((group, lanes, span), lambda s: (s, 0, 0)),
        scratch_shapes=[
            pltpu.VMEM((columns, group * span), jnp.bfloat16),
            pltpu.VMEM((lanes, span), jnp.float32),
        ],
        compiler_params=pltpu.CompilerParams(vmem_limit_bytes=5 * MIB),
        cost_estimate=work(0.2),
        name="spread_modes",
    )(modes, after)


def grad_kernel(chunk, chunks, depth, firsts, aliased, modes_ref, *refs):
    count = 1 + max(index for index, _ in firsts)
    out_hbm, other_ref, own_ref, sems = refs[count + aliased :]
    half_rows = modes_ref.shape[1] // 2
    kept, size, width = other_ref.shape
    half = width // 2
    core = lax.rem(lax.axis_index("dp"), 2)
    first = core == 0
    group = min(16, size // depth)
    tile = group * depth
    steps = size // tile

    def write(s):
        start = pl.multiple_of(s * tile, tile)
        place = pl.multiple_of((core * chunks + chunk) * size + s * tile, tile)
        return pltpu.make_async_copy(
            own_ref.at[:, pl.ds(start, tile), :], out_hbm.at[:, pl.ds(place, tile), :], sems.at[s]
        )

    for s in range(steps):
        for g in range(group):
            start = s * tile + g * depth
            right = jnp.concatenate(
                [refs[i][at + start : at + start + depth, :] for i, at in firsts], axis=0
            )
            left = modes_ref[(chunk * steps + s) * group + g]
            both = jnp.dot(left, right, preferred_element_type=jnp.float32)
            plain, turned = both[:half_rows], both[half_rows:]
            total = plain + jnp.concatenate([turned[:, half:], -turned[:, :half]], axis=1)
            low, high = total[: half_rows // 2], total[half_rows // 2 :]
            own, other = jnp.where(first, low, high), jnp.where(first, high, low)
            for i in range(kept):
                own_ref[i, pl.ds(start, depth), :] = own[i * depth : (i + 1) * depth]
                other_ref[i, pl.ds(start, depth), :] = other[i * depth : (i + 1) * depth]
        write(s).start()
    for s in range(steps):
        write(s).wait()


def grad_chunk(modes, rows, kept, depth, chunk, chunks, previous):
    arrays, firsts = [], []
    for array, first in rows:
        if not any(array is known for known in arrays):
            arrays.append(array)
        firsts.append(([array is known for known in arrays].index(True), first))
    size, width = arrays[0].shape[0] // chunks, arrays[0].shape[1]
    hbm = pl.BlockSpec(memory_space=pl.ANY)
    vmem = pl.BlockSpec(memory_space=pltpu.VMEM)
    operands = [modes, *arrays]
    in_specs = [vmem] * len(operands)
    aliases = {}
    if previous is not None:
        in_specs.append(hbm)
        aliases = {len(operands): 0}
        operands.append(previous)
    steps = size // depth // min(16, size // depth)
    return pl.pallas_call(
        functools.partial(grad_kernel, chunk, chunks, depth, firsts, int(previous is not None)),
        out_shape=[
            jax.ShapeDtypeStruct((kept, 2 * chunks * size, width), jnp.float32),
            jax.ShapeDtypeStruct((kept, size, width), jnp.float32),
        ],
        in_specs=in_specs,
        out_specs=[hbm, vmem],
        scratch_shapes=[
            pltpu.VMEM((kept, size, width), jnp.float32),
            pltpu.SemaphoreType.DMA((steps,)),
        ],
        input_output_aliases=aliases,
        compiler_params=pltpu.CompilerParams(vmem_limit_bytes=12 * MIB),
        cost_estimate=work(1),
        name="grad_chunk",
    )(*operands)


def place_kernel(chunk, chunks, part_ref, old_hbm, out_hbm, sems):
    del old_hbm
    kept, size, _ = part_ref.shape
    core = lax.rem(lax.axis_index("dp"), 2)
    start = pl.multiple_of(((1 - core) * chunks + chunk) * size, size)
    cuts = sems.shape[0] // kept
    rows = size // cuts
    copies = [
        pltpu.make_async_copy(
            part_ref.at[i, pl.ds(c * rows, rows), :],
            out_hbm.at[i, pl.ds(start + c * rows, rows), :],
            sems.at[i * cuts + c],
        )
        for i in range(kept)
        for c in range(cuts)
    ]
    for copy in copies:
        copy.start()
    for copy in copies:
        copy.wait()


def place_chunk(part, result, chunk, chunks):
    hbm = pl.BlockSpec(memory_space=pl.ANY)
    return pl.pallas_call(
        functools.partial(place_kernel, chunk, chunks),
        out_shape=jax.ShapeDtypeStruct(result.shape, result.dtype),
        in_specs=[pl.BlockSpec(memory_space=pltpu.VMEM), hbm],
        out_specs=hbm,
        scratch_shapes=[pltpu.SemaphoreType.DMA((part.shape[0],))],
        input_output_aliases={1: 0},
        compiler_params=pltpu.CompilerParams(vmem_limit_bytes=2 * MIB),
        cost_estimate=work(0.2),
        name="place_chunk",
    )(part, result)


def cast_kernel(parts, rows_hbm, keep_ref, give_ref, held_ref, sems):
    size = held_ref.shape[0] // (2 * parts)
    core = lax.rem(lax.axis_index("dp"), 2)
    halves = [(keep_ref, core * parts), (give_ref, (1 - core) * parts)]
    copies, jobs = [], []
    for h, (out, first) in enumerate(halves):
        for i in range(parts):
            source = pl.ds(pl.multiple_of((first + i) * size, size), size)
            spot = pl.ds((h * parts + i) * size, size)
            copies.append(
                pltpu.make_async_copy(
                    rows_hbm.at[source, :], held_ref.at[spot, :], sems.at[h * parts + i]
                )
            )
            jobs.append((out, pl.ds(i * size, size), spot))
    for copy in copies:
        copy.start()
    for copy, (out, place, spot) in zip(copies, jobs):
        copy.wait()
        out[place, :] = held_ref[spot, :].astype(jnp.bfloat16)


def cast_rows(rows):
    parts = 2
    total, width = rows.shape
    return pl.pallas_call(
        functools.partial(cast_kernel, parts),
        out_shape=[jax.ShapeDtypeStruct((total // 2, width), jnp.bfloat16)] * 2,
        in_specs=[pl.BlockSpec(memory_space=pltpu.HBM)],
        out_specs=[pl.BlockSpec(memory_space=pltpu.VMEM)] * 2,
        scratch_shapes=[
            pltpu.VMEM(rows.shape, jnp.float32),
            pltpu.SemaphoreType.DMA((2 * parts,)),
        ],
        compiler_params=pltpu.CompilerParams(vmem_limit_bytes=8 * MIB),
        cost_estimate=work(0.1),
        name="cast_rows",
    )(*in_hbm(rows))


def chip_ring(chips):
    order = list(range(0, chips, 2))
    return order + [c for c in range(chips - 1, 0, -1) if c % 2]


def ring_perm(chips, step):
    order = chip_ring(chips)
    return [
        (2 * order[p] + core, 2 * order[(p + step) % chips] + core)
        for p in range(chips)
        for core in (0, 1)
    ]


def ring_chip(chip, p, chips):
    up = (chips + 1) // 2
    place = jnp.where(lax.rem(chip, 2) == 0, lax.div(chip, 2), chips - 1 - lax.div(chip, 2))
    spot = lax.rem(place - p + chips, chips)
    return jnp.where(spot < up, 2 * spot, 2 * (chips - 1 - spot) + 1)


def joint_kernel(spans, total, *refs):
    for parts, new in zip(spans, refs[total:]):
        place = 0
        for source, start, size in parts:
            new[place : place + size] = refs[source][start : start + size]
            place += size


def joint(pieces, *after):
    arrays, spans = [], []

    def known(array):
        for i, other in enumerate(arrays):
            if other is array:
                return i
        arrays.append(array)
        return len(arrays) - 1

    for piece in pieces:
        parts = piece if isinstance(piece, list) else [piece]
        parts = [p if isinstance(p, tuple) else (p, 0, p.shape[0]) for p in parts]
        spans.append([(known(array), start, size) for array, start, size in parts])
    vmem = pl.BlockSpec(memory_space=pltpu.VMEM)
    operands = [*arrays, *after]
    return pl.pallas_call(
        functools.partial(joint_kernel, spans, len(operands)),
        out_shape=[
            jax.ShapeDtypeStruct(
                (sum(part[2] for part in parts), *arrays[parts[0][0]].shape[1:]),
                arrays[parts[0][0]].dtype,
            )
            for parts in spans
        ],
        in_specs=[vmem] * len(operands),
        out_specs=[vmem] * len(spans),
        compiler_params=pltpu.CompilerParams(vmem_limit_bytes=2 * MIB),
        cost_estimate=work(0.01),
        name="joint",
    )(*operands)


def per_device(
    point_feats, point_coords, slot_block, slot_cell, slot_count, cotangent, offset_map,
    offset_bias, kernel_mix, lift_weight,
):
    slabs = lax.axis_size("slab")
    devices = lax.axis_size("dp")
    channels = point_feats.shape[2]
    mode_count = cotangent.shape[2]
    capacity = slot_block.shape[3]
    width = cotangent.shape[4]
    planes = GX // slabs
    kept = channels // devices
    slots = slabs * slabs * capacity
    local_x = cotangent.shape[1]
    total = local_x // 2 * mode_count
    chunks = 2
    group = min(8, total // chunks)
    chips = devices // 2
    far = chips // 2

    scale = 1.0 / math.sqrt(GZ * slabs * slabs * capacity)

    def up(rows):
        return lax.ppermute(rows, "dp", ring_perm(chips, 1))

    def down(rows):
        return lax.ppermute(rows, "dp", ring_perm(chips, -1))

    def swap(rows):
        return lax.ppermute(rows, "dp", [(d, d ^ 1) for d in range(devices)])

    own, given = cast_rows(cotangent[0].reshape(-1, width))
    size = own.shape[0]
    ups, downs = [up(own)], [down(own)]
    twin = swap(given)
    ups.append(up(twin))
    downs.append(down(twin))

    sent = slot_terms(
        slot_block[0, 0], slot_cell[0, 0], slot_count[0, 0], point_feats[0],
        jnp.swapaxes(point_coords[0], 0, 1), offset_map.T, offset_bias[None], kernel_mix, planes,
        twin,
    )
    pair = {}
    outs = joint([*ups, *downs], sent[0])
    pair[1], pair[chips - 1] = outs[:2], outs[2:]

    pair[2] = [up(rows) for rows in pair[1]]
    pair[chips - 2] = [down(rows) for rows in pair[chips - 1]]
    terms = [list(sent)] + [
        [lax.ppermute(x, "slab", [(t, (t + s) % slabs) for t in range(slabs)]) for x in sent]
        for s in range(1, slabs)
    ]
    terms = joint(terms)
    payload, lift_done = lift_slots(terms, lift_weight, capacity, chips, mode_count)
    recv = lax.all_to_all(
        payload.reshape(chips, -1, GZ), "dp", split_axis=0, concat_axis=0, tiled=True,
        axis_index_groups=[list(range(c, devices, 2)) for c in range(2)],
    ).reshape(payload.shape)
    outs = joint([pair[2][0], pair[chips - 2][0]], lift_done)
    sent_on = {2: [outs[0], pair[2][1]], chips - 2: [outs[1], pair[chips - 2][1]]}

    for s in range(3, far):
        pair[s] = [up(rows) for rows in sent_on.get(s - 1, pair[s - 1])]
        pair[chips - s] = [
            down(rows) for rows in sent_on.get(chips - s + 1, pair[chips - s + 1])
        ]
    modes, modes_done = sample_modes(
        [recv, swap(recv)], chips, slabs, slots, planes, scale, group, total, mode_count,
        4 * kept * mode_count,
    )
    half = size // 2
    first, second = joint(
        [
            [(rows, 0, half) for rows in pair[far - 1]],
            [(rows, half, half) for rows in pair[far + 1]],
        ],
        modes_done,
    )

    pair[2][1], pair[chips - 2][1] = joint([pair[2][1], pair[chips - 2][1]], modes_done)

    ends = [up(first), down(second)]
    modes = spread_modes(modes, group, mode_count, first)

    result, parts = None, []
    for c in range(chunks):
        rows = [(own, c * half), (twin, c * half)]
        for p in range(1, chips):
            if p == far:
                rows += [(ends[c], 0), (ends[c], half)]
            else:
                rows += [(array, c * half) for array in pair[p]]
        result, part = grad_chunk(modes, rows, kept, mode_count, c, chunks, result)
        parts.append(swap(part))
    for c, part in enumerate(parts):
        result = place_chunk(part, result, c, chunks)
    return result.reshape(kept, local_x, mode_count, mode_count, width)


def solution(mesh):
    placed = (
        P("dp", "slab", None, None),
        P("dp", "slab", None, None),
        P("dp", "slab", None, None),
        P("dp", "slab", None, None),
        P("dp", "slab", None),
        P("dp", "slab", None, None, None),
        P(),
        P(),
        P(),
        P(),
    )
    return jax.shard_map(
        per_device,
        mesh=mesh,
        in_specs=placed,
        out_specs=P("dp", "slab", None, None, None),
        check_vma=False,
    )
```

```python
import functools
import math

import jax
import jax.numpy as jnp
from jax import lax
from jax.experimental import pallas as pl
from jax.experimental.pallas import tpu as pltpu
from jax.sharding import PartitionSpec as P

GX = 128
GY = 128
GZ = 128
MIB = 1024 * 1024


def in_hbm(*arrays):
    return [pltpu.with_memory_space_constraint(a, pltpu.HBM) for a in arrays]


def work(micros):
    return pl.CostEstimate(flops=int(micros * 10**9), bytes_accessed=1024, transcendentals=0)


HIGH = lax.Precision.HIGHEST
ROWS0 = (((0,), (0,)), ((), ()))


def slot_kernel(slabs, planes, block_hbm, cell_hbm, count_hbm, feats_hbm, coords_hbm, map_hbm, bias_hbm, mix_hbm, after_hbm, *refs):
    del after_hbm
    outs = refs[:2]
    (block_ref, cell_ref, count_ref, feats_ref, coords_ref, map_ref, bias_ref, mix_ref, list_ref,
     turned_ref, mixed_ref, part_ref, coef_ref, out_ref, acc_ref, spot_ref, sems) = refs[2:]
    me = lax.axis_index("slab")
    pairs = [(block_hbm, block_ref), (cell_hbm, cell_ref), (count_hbm, count_ref), (feats_hbm, feats_ref),
             (coords_hbm, coords_ref), (map_hbm, map_ref), (bias_hbm, bias_ref), (mix_hbm, mix_ref)]
    copies = [pltpu.make_async_copy(a, b, sems.at[i]) for i, (a, b) in enumerate(pairs)]
    for c in copies: c.start()
    capacity = block_ref.shape[1]
    blocks, channels, points = feats_ref.shape
    hidden = mix_ref.shape[0]
    width = blocks * channels
    base = capacity * channels + 8
    row8 = lax.broadcasted_iota(jnp.int32, (8, points), 0)
    pos_z = (lax.broadcasted_iota(jnp.int32, (GZ, points), 0).astype(jnp.float32) + 0.5) * (1.0 / GZ)
    for c in copies[:7]: c.wait()
    spot_ref[...] = coords_ref[...].astype(jnp.float32)
    for b in range(blocks):
        turned_ref[:, b * channels : (b + 1) * channels] = feats_ref[b].astype(jnp.float32).T.astype(jnp.bfloat16)
    cat = jnp.concatenate([map_ref[...], bias_ref[...], jnp.zeros((4, hidden), jnp.float32)], axis=0)
    live = jnp.int32(0)
    sides = [jnp.where(row8 == 2, 1.0, 0.0)]
    for r in range(slabs):
        peer = lax.rem(me + r, slabs)
        tag_rows = jnp.full((8, points), -1.0, jnp.float32)
        for j in range(capacity):
            n = r * capacity + j
            block = block_ref[peer, j]
            cell = cell_ref[peer, j]
            alive = j < count_ref[peer]
            @pl.when(alive)
            def _():
                list_ref[live] = n
                list_ref[live + 1] = n
            live = live + alive.astype(jnp.int32)
            list_ref[slabs * capacity + 1 + n] = block
            pos_x = ((peer * planes + lax.div(cell, GY)).astype(jnp.float32) + 0.5) * (1.0 / GX)
            pos_y = (lax.rem(cell, GY).astype(jnp.float32) + 0.5) * (1.0 / GY)
            q0 = spot_ref[0, pl.ds(block, 1), :]
            q1 = spot_ref[1, pl.ds(block, 1), :]
            q2 = spot_ref[2, pl.ds(block, 1), :]
            side = jnp.where(row8 == 0, pos_x - q0, jnp.where(row8 == 1, pos_y - q1, jnp.where(row8 == 2, -q2, jnp.where(row8 == 3, 1.0, 0.0))))
            sides.append(side)
            tag_rows = jnp.where(row8 == j, jnp.where(alive, cell, -1).astype(jnp.float32), tag_rows)
        out_ref[r * base + capacity * channels : (r + 1) * base, :] = tag_rows
    parts = lax.dot_general(
        cat, jnp.concatenate(sides, axis=1), ROWS0, precision=HIGH,
        preferred_element_type=jnp.float32,
    )
    coef_ref[...] = parts[:, :points]
    for n in range(slabs * capacity):
        part_ref[n] = parts[:, (n + 1) * points : (n + 2) * points]
    copies[7].wait()
    lane = lax.broadcasted_iota(jnp.int32, (channels, 2 * channels), 1)
    left = turned_ref[...]

    step = max(1, min(hidden // 2, 512 // (blocks * blocks)))

    def mix_step(it, carry):
        for u in range(step):
            h = it * step + u
            mix = mix_ref[h]
            wide = jnp.concatenate([mix, mix], axis=1)
            zero = jnp.zeros_like(wide)
            halves = (jnp.where(lane < channels, wide, zero), jnp.where(lane < channels, zero, wide))
            rows = [jnp.concatenate([halves[b % 2] if b // 2 == t else zero for t in range(blocks // 2)], axis=1) for b in range(blocks)]
            mixed_ref[pl.ds(pl.multiple_of(h * points, points), points), :] = jnp.dot(left, jnp.concatenate(rows, axis=0), preferred_element_type=jnp.float32).astype(jnp.bfloat16)
        return carry
    lax.fori_loop(0, hidden // step, mix_step, 0)

    def pair(it, carry):
        ids = [list_ref[2 * it], list_ref[2 * it + 1]]
        part = 8
        for k in range(0, hidden, part):
            cols = []
            for h in range(k, k + part):
                cell_z = pos_z * coef_ref[h : h + 1, :]
                cols.append(jnp.concatenate([jnp.maximum(cell_z + part_ref[n, h : h + 1, :], 0.0).astype(jnp.bfloat16) for n in ids], axis=0))
            got = jnp.dot(jnp.concatenate(cols, axis=1), mixed_ref[k * points : (k + part) * points, :], preferred_element_type=jnp.float32)
            if k: acc_ref[...] += got
            else: acc_ref[...] = got
        for j, n in enumerate(ids):
            block = list_ref[slabs * capacity + 1 + n]
            pick = acc_ref[j * GZ : (j + 1) * GZ, : 2 * channels]
            for t in range(1, blocks // 2):
                pick = jnp.where(block // 2 == t, acc_ref[j * GZ : (j + 1) * GZ, 2 * t * channels : 2 * (t + 1) * channels], pick)
            turned = pick.T * (1.0 / points)
            start = pl.multiple_of((n // capacity) * base + (n % capacity) * channels, 8)
            out_ref[pl.ds(start, channels), :] = jnp.where(block % 2 == 1, turned[channels:], turned[:channels])
        return carry
    lax.fori_loop(0, (live + 1) // 2, pair, 0)
    for i, out in enumerate(outs):
        out[...] = out_ref[i * out.shape[0] : (i + 1) * out.shape[0], :]

def slot_terms(slot_block, slot_cell, slot_count, feats, coords, offset_map, offset_bias, kernel_mix, planes, after):
    slabs, capacity = slot_block.shape
    blocks, channels, points = feats.shape
    hidden = kernel_mix.shape[0]
    base = capacity * channels + 8
    slots = slabs * capacity
    width = blocks * channels
    slot_limit = hidden * points * width * 2 + (10 if blocks <= 4 else 24) * MIB
    hbm = pl.BlockSpec(memory_space=pltpu.HBM)
    vmem = pl.BlockSpec(memory_space=pltpu.VMEM)
    return pl.pallas_call(
        functools.partial(slot_kernel, slabs, planes),
        out_shape=[jax.ShapeDtypeStruct((slabs * base // 2, GZ), jnp.float32)] * 2,
        in_specs=[hbm] * 8 + [pl.BlockSpec(memory_space=pl.ANY)],
        out_specs=[vmem] * 2,
        scratch_shapes=[
            pltpu.SMEM((slabs, capacity), jnp.int32), pltpu.SMEM((slabs, capacity), jnp.int32), pltpu.SMEM((slabs,), jnp.int32),
            pltpu.VMEM(feats.shape, feats.dtype), pltpu.VMEM(coords.shape, coords.dtype), pltpu.VMEM(offset_map.shape, jnp.float32),
            pltpu.VMEM(offset_bias.shape, jnp.float32), pltpu.VMEM(kernel_mix.shape, kernel_mix.dtype),
            pltpu.SMEM((2 * slots + 2,), jnp.int32),
            pltpu.VMEM((points, width), jnp.bfloat16), pltpu.VMEM((hidden * points, width), jnp.bfloat16),
            pltpu.VMEM((slots, hidden, points), jnp.float32), pltpu.VMEM((hidden, points), jnp.float32),
            pltpu.VMEM((slabs * base, GZ), jnp.float32), pltpu.VMEM((2 * GZ, width), jnp.float32), pltpu.VMEM(coords.shape, jnp.float32),
            pltpu.SemaphoreType.DMA((8,)),
        ],
        compiler_params=pltpu.CompilerParams(vmem_limit_bytes=slot_limit),
        cost_estimate=work(1),
        name="slot_terms",
    )(*in_hbm(slot_block, slot_cell, slot_count, feats, coords, offset_map, offset_bias, kernel_mix),
      after)


def lift_kernel(slabs, capacity, dests, mode_count, *refs):
    terms = refs[:slabs]
    lift_ref, out_ref, token_ref, tag_ref, row_ref, wide_ref, table_ref = refs[slabs:]
    token_ref[...] = jnp.zeros_like(token_ref)
    channels = lift_ref.shape[0]
    kept = channels // dests
    group = slabs * capacity
    slots = slabs * group
    base = capacity * channels + 8
    lanes = table_ref.shape[1]
    tiles = lanes // GZ
    per = out_ref.shape[0] // dests
    cells = lax.broadcasted_iota(jnp.int32, (GZ, lanes), 0)
    lane = lax.broadcasted_iota(jnp.int32, (GZ, lanes), 1)
    step = cells * (lane % mode_count) + jnp.where(lane >= lanes // 2, GZ // 4, 0)
    waves = jnp.cos((step % GZ).astype(jnp.float32) * (2.0 * math.pi / GZ))
    for i in range(kept):
        mine = lane // mode_count % kept == i
        table_ref[i * GZ : (i + 1) * GZ, :] = jnp.where(mine, waves, 0.0)

    def receiver(u, carry):
        starts = [lax.rem(u + s, slabs) * base for s in range(slabs)]

        def tag_of(m):
            first = pl.multiple_of(starts[m // capacity] + capacity * channels, 8)
            return terms[m // capacity][pl.ds(first, 8), :][m % capacity : m % capacity + 1, :]

        def terms_of(m):
            first = pl.multiple_of(starts[m // capacity] + (m % capacity) * channels, 8)
            return terms[m // capacity][pl.ds(first, channels), :]

        tags = [tag_of(m) for m in range(group)]
        for n in range(group):
            live = tags[n] >= 0.0
            summed = jnp.zeros((channels, GZ), jnp.float32)
            leader = live
            for m in range(group):
                same = (tags[m] == tags[n]) & live
                summed = summed + jnp.where(same, terms_of(m), 0.0)
                if m < n:
                    leader = leader & jnp.logical_not(same)
            latent = summed.astype(jnp.bfloat16)
            lifted = jax.nn.gelu(
                lax.dot_general(lift_ref[...], latent, ROWS0, preferred_element_type=jnp.float32)
            )
            row_ref[n] = jnp.where(leader, lifted, 0.0)
            rows = pl.ds(pl.multiple_of((u * group + n) * dests, 8), dests)
            for i in range(kept):
                wide_ref[rows, i * GZ : (i + 1) * GZ] = row_ref[
                    n, pl.ds(i, dests, stride=kept), :
                ]
        tag_ref[pl.ds(pl.multiple_of(u * group, 8), group), :] = jnp.concatenate(tags, axis=0)
        return carry

    lax.fori_loop(0, slabs, receiver, 0, unroll=slabs <= 2)
    modes = jnp.dot(
        wide_ref[...], table_ref[...], precision=HIGH, preferred_element_type=jnp.float32
    )
    for n in range(slots):
        for t in range(tiles):
            out_ref[pl.ds(t * slots + n, dests, stride=per), :] = modes[
                n * dests : (n + 1) * dests, t * GZ : (t + 1) * GZ
            ]
    row = lax.broadcasted_iota(jnp.int32, (slots, GZ), 0)
    lane = lax.broadcasted_iota(jnp.int32, (slots, GZ), 1)
    place = lax.broadcasted_iota(jnp.int32, (8, GZ), 0)
    packed = jnp.zeros((8, GZ), jnp.float32)
    for k in range((slots + GZ - 1) // GZ):
        line = jnp.sum(jnp.where(row == lane + k * GZ, tag_ref[...], 0.0), axis=0, keepdims=True)
        packed = jnp.where(place == k, line, packed)
    for d in range(dests):
        out_ref[d * per + tiles * slots : (d + 1) * per, :] = packed


def lift_slots(terms, lift_weight, capacity, dests, mode_count):
    slabs = len(terms)
    channels = lift_weight.shape[0]
    slots = slabs * slabs * capacity
    kept = channels // dests
    lanes = 2 * kept * mode_count
    per = lanes // GZ * slots + 8
    vmem = pl.BlockSpec(memory_space=pltpu.VMEM)
    return pl.pallas_call(
        functools.partial(lift_kernel, slabs, capacity, dests, mode_count),
        out_shape=[
            jax.ShapeDtypeStruct((dests * per, GZ), jnp.float32),
            jax.ShapeDtypeStruct((8, GZ), jnp.float32),
        ],
        in_specs=[vmem] * (slabs + 1),
        out_specs=[vmem] * 2,
        scratch_shapes=[
            pltpu.VMEM((slots, GZ), jnp.float32),
            pltpu.VMEM((slabs * capacity, channels, GZ), jnp.float32),
            pltpu.VMEM((slots * dests, kept * GZ), jnp.float32),
            pltpu.VMEM((kept * GZ, lanes), jnp.float32),
        ],
        compiler_params=pltpu.CompilerParams(
            vmem_limit_bytes=(6 if slabs <= 2 else 48) * MIB
        ),
        cost_estimate=work(0.1),
        name="lift_slots",
    )(*terms, lift_weight)


def modes_kernel(chips, slabs, slots, planes, scale, group, mode_count, *refs):
    recv_refs = refs[:2]
    out_ref, token_ref, all_ref = refs[2:]
    token_ref[...] = jnp.zeros_like(token_ref)
    samples = 2 * chips
    tiles = all_ref.shape[0]
    total = all_ref.shape[1] // samples
    half = tiles * GZ // 2
    per = recv_refs[0].shape[0] // chips

    device = lax.axis_index("dp")
    slab = lax.axis_index("slab")
    first_x = (slab * 2 + lax.rem(device, 2)) * (total // mode_count)
    spot = lax.broadcasted_iota(jnp.int32, (1, total), 1)
    freq_x = first_x + spot // mode_count
    freq_y = spot % mode_count
    freq_x = jnp.where(freq_x < mode_count // 2, freq_x, freq_x - mode_count)
    freq_y = jnp.where(freq_y < mode_count // 2, freq_y, freq_y - mode_count)
    freq_x, freq_y = freq_x.astype(jnp.float32), freq_y.astype(jnp.float32)

    row = lax.broadcasted_iota(jnp.int32, (slots, GZ), 0)
    lane = lax.broadcasted_iota(jnp.int32, (slots, GZ), 1)
    peer = slab + lax.broadcasted_iota(jnp.int32, (slots, 1), 0) // (slots // slabs)
    plane = jnp.where(peer >= slabs, peer - slabs, peer).astype(jnp.float32) * planes

    def body(p, carry):
        base = pl.multiple_of(ring_chip(lax.div(device, 2), p, chips) * per, 8)
        for core, ref in enumerate(recv_refs):
            plain = jnp.concatenate(
                [ref[pl.ds(base + u * slots, slots), :] for u in range(tiles)], axis=1
            )
            packed = ref[pl.ds(base + tiles * slots, 8), :]
            tag = jnp.zeros((slots, 1), jnp.float32)
            for k in range((slots + GZ - 1) // GZ):
                tag = tag + jnp.sum(
                    jnp.where(row == lane + k * GZ, packed[k : k + 1, :], 0.0),
                    axis=1,
                    keepdims=True,
                )
            tag = jnp.maximum(tag, 0.0)
            local_x = jnp.floor(tag * (1.0 / GY))
            turns = (local_x + plane) * (1.0 / GX) * freq_x + (
                tag - local_x * GY
            ) * (1.0 / GY) * freq_y
            angle = (turns - jnp.floor(turns)) * (2.0 * math.pi)
            crossed = jnp.concatenate([plain[:, half:], -plain[:, :half]], axis=1)
            modes = lax.dot_general(
                jnp.concatenate([jnp.cos(angle), jnp.sin(angle)], axis=0),
                jnp.concatenate([plain, crossed], axis=0),
                ROWS0,
                precision=HIGH,
                preferred_element_type=jnp.float32,
            )
            for u in range(tiles):
                all_ref[u, pl.ds(2 * p + core, total, stride=samples), :] = (
                    modes[:, u * GZ : (u + 1) * GZ] * scale
                )
        return carry

    lax.fori_loop(0, chips, body, 0, unroll=4)

    span = group * samples
    for block in range(total // group):
        for u in range(tiles):
            out_ref[block, u * GZ : (u + 1) * GZ, :] = all_ref[
                u, block * span : (block + 1) * span, :
            ].T.astype(jnp.bfloat16)


def sample_modes(recv, chips, slabs, slots, planes, scale, group, total, mode_count, lanes):
    samples = 2 * chips
    vmem = pl.BlockSpec(memory_space=pltpu.VMEM)
    return pl.pallas_call(
        functools.partial(modes_kernel, chips, slabs, slots, planes, scale, group, mode_count),
        out_shape=[
            jax.ShapeDtypeStruct((total // group, lanes, group * samples), jnp.bfloat16),
            jax.ShapeDtypeStruct((8, GZ), jnp.float32),
        ],
        in_specs=[vmem] * len(recv),
        out_specs=[vmem] * 2,
        scratch_shapes=[pltpu.VMEM((lanes // GZ, total * samples, GZ), jnp.float32)],
        compiler_params=pltpu.CompilerParams(vmem_limit_bytes=(5 if slabs <= 2 else 32) * MIB),
        cost_estimate=work(0.2),
        name="sample_modes",
    )(*recv)


def spread_kernel(depth, modes_ref, after_ref, out_ref, pick_ref, mask_ref):
    del after_ref
    group = out_ref.shape[0]
    span = out_ref.shape[2]

    @pl.when(pl.program_id(0) == 0)
    def _():
        row = lax.broadcasted_iota(jnp.int32, pick_ref.shape, 0)
        col = lax.broadcasted_iota(jnp.int32, pick_ref.shape, 1)
        pick_ref[...] = jnp.where(row == col // depth, 1.0, 0.0).astype(jnp.bfloat16)
        row = lax.broadcasted_iota(jnp.int32, mask_ref.shape, 0)
        col = lax.broadcasted_iota(jnp.int32, mask_ref.shape, 1)
        mask_ref[...] = jnp.where(row % depth == col % depth, 1.0, 0.0)

    for g in range(group):
        left = jnp.dot(
            modes_ref[0], pick_ref[:, g * span : (g + 1) * span],
            preferred_element_type=jnp.float32,
        )
        out_ref[g] = (left * mask_ref[...]).astype(jnp.bfloat16)


def spread_modes(modes, group, depth, after):
    blocks, lanes, columns = modes.shape
    span = columns // group * depth
    return pl.pallas_call(
        functools.partial(spread_kernel, depth),
        out_shape=jax.ShapeDtypeStruct((blocks * group, lanes, span), jnp.bfloat16),
        grid=(blocks,),
        in_specs=[
            pl.BlockSpec((1, lanes, columns), lambda s: (s, 0, 0)),
            pl.BlockSpec(memory_space=pl.ANY),
        ],
        out_specs=pl.BlockSpec((group, lanes, span), lambda s: (s, 0, 0)),
        scratch_shapes=[
            pltpu.VMEM((columns, group * span), jnp.bfloat16),
            pltpu.VMEM((lanes, span), jnp.float32),
        ],
        compiler_params=pltpu.CompilerParams(vmem_limit_bytes=5 * MIB),
        cost_estimate=work(0.2),
        name="spread_modes",
    )(modes, after)


def grad_kernel(chunks, size, depth, firsts, mine, modes_ref, *refs):
    count = 1 + max(index for places in firsts for index, _ in places)
    if mine:
        out_hbm, held_ref, sems = refs[count:]
    else:
        held_ref = refs[count]
    half_rows = modes_ref.shape[1] // 2
    part_rows = half_rows // 2
    kept, _, width = held_ref.shape
    half = width // 2
    core = lax.rem(lax.axis_index("dp"), 2)
    head = core if mine else 1 - core
    group = min(16, size // depth)
    tile = group * depth
    steps = size // tile
    copies = []
    for n, (chunk, places) in enumerate(zip(chunks, firsts)):
        for s in range(steps):
            for g in range(group):
                start = s * tile + g * depth
                right = jnp.concatenate(
                    [refs[i][at + start : at + start + depth, :] for i, at in places], axis=0
                )
                index = (chunk * steps + s) * group + g
                left = jnp.concatenate(
                    [
                        modes_ref[
                            index,
                            pl.ds(
                                pl.multiple_of(p * half_rows + head * part_rows, part_rows),
                                part_rows,
                            ),
                            :,
                        ]
                        for p in range(2)
                    ],
                    axis=0,
                )
                both = jnp.dot(left, right, preferred_element_type=jnp.float32)
                plain, turned = both[:part_rows], both[part_rows:]
                total = plain + jnp.concatenate([turned[:, half:], -turned[:, :half]], axis=1)
                for i in range(kept):
                    held_ref[i, n * size + start : n * size + start + depth, :] = total[
                        i * depth : (i + 1) * depth
                    ]
            if mine:
                place = pl.multiple_of(core * (len(chunks) * size) + n * size + s * tile, tile)
                copies.append(
                    pltpu.make_async_copy(
                        held_ref.at[:, n * size + s * tile : n * size + (s + 1) * tile, :],
                        out_hbm.at[:, pl.ds(place, tile), :],
                        sems.at[n * steps + s],
                    )
                )
                copies[-1].start()
    for copy in copies:
        copy.wait()


def grad_rows(modes, rows, kept, depth, chunks, mine):
    arrays, firsts = [], []
    for part in rows:
        firsts.append([])
        for array, first in part:
            if not any(array is known for known in arrays):
                arrays.append(array)
            firsts[-1].append(([array is known for known in arrays].index(True), first))
    size, width = arrays[0].shape[0] // 2, arrays[0].shape[1]
    vmem = pl.BlockSpec(memory_space=pltpu.VMEM)
    shape = (kept, len(chunks) * size, width)
    steps = size // depth // min(16, size // depth)
    return pl.pallas_call(
        functools.partial(grad_kernel, chunks, size, depth, firsts, mine),
        out_shape=jax.ShapeDtypeStruct(
            (kept, 2 * shape[1], width) if mine else shape, jnp.float32
        ),
        in_specs=[vmem] * (1 + len(arrays)),
        out_specs=pl.BlockSpec(memory_space=pl.ANY) if mine else vmem,
        scratch_shapes=[
            pltpu.VMEM(shape, jnp.float32),
            pltpu.SemaphoreType.DMA((len(chunks) * steps,)),
        ] if mine else [],
        compiler_params=pltpu.CompilerParams(vmem_limit_bytes=14 * MIB),
        cost_estimate=work(1),
        name="grad_rows",
    )(modes, *arrays)


def place_kernel(chunk, chunks, part_ref, old_hbm, out_hbm, sems):
    del old_hbm
    kept, size, _ = part_ref.shape
    core = lax.rem(lax.axis_index("dp"), 2)
    start = pl.multiple_of(((1 - core) * chunks + chunk) * size, size)
    cuts = sems.shape[0] // kept
    rows = size // cuts
    copies = [
        pltpu.make_async_copy(
            part_ref.at[i, pl.ds(c * rows, rows), :],
            out_hbm.at[i, pl.ds(start + c * rows, rows), :],
            sems.at[i * cuts + c],
        )
        for i in range(kept)
        for c in range(cuts)
    ]
    for copy in copies:
        copy.start()
    for copy in copies:
        copy.wait()


def place_chunk(part, result, chunk, chunks):
    hbm = pl.BlockSpec(memory_space=pl.ANY)
    return pl.pallas_call(
        functools.partial(place_kernel, chunk, chunks),
        out_shape=jax.ShapeDtypeStruct(result.shape, result.dtype),
        in_specs=[pl.BlockSpec(memory_space=pltpu.VMEM), hbm],
        out_specs=hbm,
        scratch_shapes=[pltpu.SemaphoreType.DMA((part.shape[0],))],
        input_output_aliases={1: 0},
        compiler_params=pltpu.CompilerParams(vmem_limit_bytes=2 * MIB),
        cost_estimate=work(0.2),
        name="place_chunk",
    )(part, result)


def cast_kernel(parts, rows_hbm, keep_ref, give_ref, held_ref, sems):
    size = held_ref.shape[0] // (2 * parts)
    core = lax.rem(lax.axis_index("dp"), 2)
    halves = [(keep_ref, core * parts), (give_ref, (1 - core) * parts)]
    copies, jobs = [], []
    for h, (out, first) in enumerate(halves):
        for i in range(parts):
            source = pl.ds(pl.multiple_of((first + i) * size, size), size)
            spot = pl.ds((h * parts + i) * size, size)
            copies.append(
                pltpu.make_async_copy(
                    rows_hbm.at[source, :], held_ref.at[spot, :], sems.at[h * parts + i]
                )
            )
            jobs.append((out, pl.ds(i * size, size), spot))
    for copy in copies:
        copy.start()
    for copy, (out, place, spot) in zip(copies, jobs):
        copy.wait()
        out[place, :] = held_ref[spot, :].astype(jnp.bfloat16)


def cast_rows(rows):
    parts = 2
    total, width = rows.shape
    return pl.pallas_call(
        functools.partial(cast_kernel, parts),
        out_shape=[jax.ShapeDtypeStruct((total // 2, width), jnp.bfloat16)] * 2,
        in_specs=[pl.BlockSpec(memory_space=pltpu.HBM)],
        out_specs=[pl.BlockSpec(memory_space=pltpu.VMEM)] * 2,
        scratch_shapes=[
            pltpu.VMEM(rows.shape, jnp.float32),
            pltpu.SemaphoreType.DMA((2 * parts,)),
        ],
        compiler_params=pltpu.CompilerParams(vmem_limit_bytes=8 * MIB),
        cost_estimate=work(0.1),
        name="cast_rows",
    )(*in_hbm(rows))


def chip_ring(chips):
    order = list(range(0, chips, 2))
    return order + [c for c in range(chips - 1, 0, -1) if c % 2]


def ring_perm(chips, step):
    order = chip_ring(chips)
    return [
        (2 * order[p] + core, 2 * order[(p + step) % chips] + core)
        for p in range(chips)
        for core in (0, 1)
    ]


def ring_chip(chip, p, chips):
    up = (chips + 1) // 2
    place = jnp.where(lax.rem(chip, 2) == 0, lax.div(chip, 2), chips - 1 - lax.div(chip, 2))
    spot = lax.rem(place - p + chips, chips)
    return jnp.where(spot < up, 2 * spot, 2 * (chips - 1 - spot) + 1)


def joint_kernel(spans, total, *refs):
    for parts, new in zip(spans, refs[total:]):
        place = 0
        for source, start, size in parts:
            new[place : place + size] = refs[source][start : start + size]
            place += size


def joint(pieces, *after):
    arrays, spans = [], []

    def known(array):
        for i, other in enumerate(arrays):
            if other is array:
                return i
        arrays.append(array)
        return len(arrays) - 1

    for piece in pieces:
        parts = piece if isinstance(piece, list) else [piece]
        parts = [p if isinstance(p, tuple) else (p, 0, p.shape[0]) for p in parts]
        spans.append([(known(array), start, size) for array, start, size in parts])
    vmem = pl.BlockSpec(memory_space=pltpu.VMEM)
    operands = [*arrays, *after]
    return pl.pallas_call(
        functools.partial(joint_kernel, spans, len(operands)),
        out_shape=[
            jax.ShapeDtypeStruct(
                (sum(part[2] for part in parts), *arrays[parts[0][0]].shape[1:]),
                arrays[parts[0][0]].dtype,
            )
            for parts in spans
        ],
        in_specs=[vmem] * len(operands),
        out_specs=[vmem] * len(spans),
        compiler_params=pltpu.CompilerParams(vmem_limit_bytes=2 * MIB),
        cost_estimate=work(0.01),
        name="joint",
    )(*operands)


def per_device(
    point_feats, point_coords, slot_block, slot_cell, slot_count, cotangent, offset_map,
    offset_bias, kernel_mix, lift_weight,
):
    slabs = lax.axis_size("slab")
    devices = lax.axis_size("dp")
    channels = point_feats.shape[2]
    mode_count = cotangent.shape[2]
    capacity = slot_block.shape[3]
    width = cotangent.shape[4]
    planes = GX // slabs
    kept = channels // devices
    slots = slabs * slabs * capacity
    local_x = cotangent.shape[1]
    total = local_x // 2 * mode_count
    chunks = 2
    group = min(8, total // chunks)
    chips = devices // 2
    far = chips // 2

    scale = 1.0 / math.sqrt(GZ * slabs * slabs * capacity)

    def up(rows):
        return lax.ppermute(rows, "dp", ring_perm(chips, 1))

    def down(rows):
        return lax.ppermute(rows, "dp", ring_perm(chips, -1))

    def swap(rows):
        return lax.ppermute(rows, "dp", [(d, d ^ 1) for d in range(devices)])

    own, given = cast_rows(cotangent[0].reshape(-1, width))
    size = own.shape[0]
    ups, downs = [up(own)], [down(own)]
    twin = swap(given)
    ups.append(up(twin))
    downs.append(down(twin))

    sent = slot_terms(
        slot_block[0, 0], slot_cell[0, 0], slot_count[0, 0], point_feats[0],
        jnp.swapaxes(point_coords[0], 0, 1), offset_map.T, offset_bias[None], kernel_mix, planes,
        twin,
    )
    pair = {}
    outs = joint([*ups, *downs], sent[0])
    pair[1], pair[chips - 1] = outs[:2], outs[2:]

    pair[2] = [up(rows) for rows in pair[1]]
    pair[chips - 2] = [down(rows) for rows in pair[chips - 1]]
    terms = [list(sent)] + [
        [lax.ppermute(x, "slab", [(t, (t + s) % slabs) for t in range(slabs)]) for x in sent]
        for s in range(1, slabs)
    ]
    terms = joint(terms)
    payload, lift_done = lift_slots(terms, lift_weight, capacity, chips, mode_count)
    recv = lax.all_to_all(
        payload.reshape(chips, -1, GZ), "dp", split_axis=0, concat_axis=0, tiled=True,
        axis_index_groups=[list(range(c, devices, 2)) for c in range(2)],
    ).reshape(payload.shape)
    outs = joint([pair[2][0], pair[chips - 2][0]], lift_done)
    sent_on = {2: [outs[0], pair[2][1]], chips - 2: [outs[1], pair[chips - 2][1]]}

    for s in range(3, far):
        pair[s] = [up(rows) for rows in sent_on.get(s - 1, pair[s - 1])]
        pair[chips - s] = [
            down(rows) for rows in sent_on.get(chips - s + 1, pair[chips - s + 1])
        ]
    modes, modes_done = sample_modes(
        [recv, swap(recv)], chips, slabs, slots, planes, scale, group, total, mode_count,
        4 * kept * mode_count,
    )
    half = size // 2
    first, second = joint(
        [
            [(rows, 0, half) for rows in pair[far - 1]],
            [(rows, half, half) for rows in pair[far + 1]],
        ],
        modes_done,
    )

    pair[2][1], pair[chips - 2][1] = joint([pair[2][1], pair[chips - 2][1]], modes_done)

    ends = [up(first), down(second)]
    modes = spread_modes(modes, group, mode_count, first)

    rows = []
    for c in range(chunks):
        rows.append([(own, c * half), (twin, c * half)])
        for p in range(1, chips):
            if p == far:
                rows[c] += [(ends[c], 0), (ends[c], half)]
            else:
                rows[c] += [(array, c * half) for array in pair[p]]
    parts = [
        swap(grad_rows(modes, rows[c : c + 1], kept, mode_count, [c], False))
        for c in range(chunks)
    ]
    result = grad_rows(modes, rows, kept, mode_count, list(range(chunks)), True)
    for c, part in enumerate(parts):
        result = place_chunk(part, result, c, chunks)
    return result.reshape(kept, local_x, mode_count, mode_count, width)


def solution(mesh):
    placed = (
        P("dp", "slab", None, None),
        P("dp", "slab", None, None),
        P("dp", "slab", None, None),
        P("dp", "slab", None, None),
        P("dp", "slab", None),
        P("dp", "slab", None, None, None),
        P(),
        P(),
        P(),
        P(),
    )
    return jax.shard_map(
        per_device,
        mesh=mesh,
        in_specs=placed,
        out_specs=P("dp", "slab", None, None, None),
        check_vma=False,
    )
```
